256 devices in a mesh: leaf: 64 (over z, x, core), panel: 4 (over y).
Axes of the slice: x: 4, y: 4, z: 8, core: 2. Of those that a mesh axis runs over, the one named last changes fastest.
Arguments:
- rhs: bfloat16 [3, 64, 64, 1024], P(None, 'leaf', None, 'panel'), may hold values from -6 to 6
- inv_diag: bfloat16 [3, 64, 1024, 1024], P(None, 'leaf', 'panel'), as said below
- coupling: bfloat16 [2, 64, 1024, 512], P(None, 'leaf', None, 'panel'), may hold values from -0.1875 to 0.1875
- row_lists: int32 [2, 64, 512], replicated, may hold values from 0 to 1023, as said below
- parents: int32 [2, 64], replicated, may hold values from 0 to 63
- counts: int32 [2, 64], replicated, may hold values from 1 to 512, as said below
Outputs:
- forward_part: bfloat16 [3, 64, 64, 1024], P(None, 'leaf', None, 'panel')
- solution: bfloat16 [3, 64, 64, 1024], P(None, 'leaf', None, 'panel')
The draws below stay inside these ranges and needn't reach their ends.
Inputs may be any that keep to these rules, and one draw needn't show every extreme that they name: `inv_diag`: each inverse diagonal block is lower triangular with a positive diagonal. `row_lists`: each slot's list names 512 different rows. `counts`: in every level some slot has all 512 columns live.
All inputs are finite; a program needn't handle non-finite values.
Results may differ from the reference program's by a relative error of at most 0.01.
Values may be sent and summed in bfloat16 or wider, within the bound.
No kernel may reach another device: no remote copies, remote signals or barrier semaphores. Data moves between devices by JAX's collectives and lax.ppermute only.
A program may use at most 64 MiB of HBM per device.

```python
import math
import jax
import jax.numpy as jnp
import numpy as np
from jax import lax

W = 1024
RHS = 64
RU = 512
LEV = 3
LEVM = 2
SLOTS = 64


def draw_inv_diag(key, part):
    first_key, second_key = jax.random.split(key)
    shape = (LEV, SLOTS, W, W)
    row_ids = lax.broadcasted_iota(jnp.int32, (W, W), 0)
    col_ids = lax.broadcasted_iota(jnp.int32, (W, W), 1)
    lower = jax.random.normal(first_key, shape, jnp.float32) * (0.6 / math.sqrt(W))
    diagonal = jax.random.uniform(second_key, shape, jnp.float32, 0.6, 1.4)
    matrix = jnp.where(row_ids > col_ids, lower, 0.0) + jnp.where(row_ids == col_ids, diagonal, 0.0)
    return matrix.astype(jnp.bfloat16)


def draw_row_lists(key, part):
    keys = jax.random.split(key, LEVM * SLOTS)
    orders = jax.vmap(lambda single: jax.random.permutation(single, W))(keys)
    return orders[:, :RU].reshape(LEVM, SLOTS, RU).astype(jnp.int32)


def draw_counts(key, part):
    first_key, second_key = jax.random.split(key)
    base = jax.random.randint(first_key, (LEVM, SLOTS), RU // 4, RU + 1, dtype=jnp.int32)
    chosen = jax.random.randint(second_key, (LEVM, 1), 0, SLOTS, dtype=jnp.int32)
    slot_ids = lax.broadcasted_iota(jnp.int32, (LEVM, SLOTS), 1)
    return jnp.where(slot_ids == chosen, RU, base).astype(jnp.int32)


def with_ends(entries, key, low, largest):
    shape = entries.shape
    spot = [jax.random.randint(jax.random.fold_in(key, axis), (), 0, shape[axis]) for axis in range(len(shape))]
    entries = entries.at[tuple(spot)].set(low)
    longest = shape.index(max(shape))
    spot[longest] = (spot[longest] + 1) % shape[longest]
    return entries.at[tuple(spot)].set(largest)


def block_scale(stream_key, dims, cuts, least, top_value):
    gain = 1.0
    for position, parts in cuts:
        heights = jax.random.uniform(jax.random.fold_in(jax.random.fold_in(stream_key, 6), position), (parts,), jnp.float32, least / len(cuts), top_value / len(cuts))
        gain = gain * jnp.repeat(jnp.exp(heights), dims[position] // parts).reshape((-1,) + (1,) * (len(dims) - 1 - position))
    return gain


def rank_table(amount, slope):
    weights = [(1 << 20) // math.isqrt(grade ** slope) + 1 for grade in range(1, amount + 1)]
    scale = 1 + sum(weights) // (1 << 30)
    return np.cumsum(np.array([max(1, weight // scale) for weight in weights]))


def skewed_ids(stream_key, shape, number_of, skew):
    listing = rank_table(number_of, skew)
    pick = jax.random.randint(jax.random.fold_in(stream_key, 1), shape, 0, int(listing[number_of - 1]))
    standing = jnp.searchsorted(jnp.asarray(listing, jnp.int32), pick, side="right")
    return jax.random.permutation(jax.random.fold_in(stream_key, 2), number_of)[standing].astype(jnp.int32)


def normal_values(stream_key, extent, deviation, bound, cuts=(), kind=jnp.bfloat16):
    gain = block_scale(stream_key, extent, cuts, -0.22, 0.18) if cuts else 1.0
    result = jax.random.normal(stream_key, extent, jnp.float32) * deviation * gain
    return jnp.minimum(jnp.maximum(result, -bound), bound).astype(kind)


def setup_inputs(seed: int = 0) -> dict:
    streams_of = jax.random.split(jax.random.key(seed), 7)
    rhs = normal_values(streams_of[0], (LEV, SLOTS, RHS, W), 1.0, 6.0, ((1, 64), (3, 4)))
    inv_diag = draw_inv_diag(jax.random.fold_in(streams_of[6], 71), 0)
    coupling = normal_values(streams_of[2], (LEVM, SLOTS, W, RU), W ** -0.5, 0.1875, ((1, 64), (3, 4)))
    row_lists = draw_row_lists(jax.random.fold_in(streams_of[6], 71), 0)
    parents = with_ends(skewed_ids(streams_of[4], (LEVM, SLOTS), SLOTS, 2), jax.random.fold_in(streams_of[4], 3), 0, SLOTS - 1).astype(jnp.int32)
    counts = draw_counts(jax.random.fold_in(streams_of[6], 71), 0)
    return dict(rhs=rhs, inv_diag=inv_diag, coupling=coupling, row_lists=row_lists, parents=parents, counts=counts)


def rows_times(pair):
    return lax.dot_general(pair[0], pair[1], (((1,), (1,)), ((), ())), preferred_element_type=jnp.float32)


def plain_times(pair):
    return jnp.dot(pair[0], pair[1], preferred_element_type=jnp.float32)


def reference(rhs, inv_diag, coupling, row_lists, parents, counts):
    column_ids = jnp.arange(RU, dtype=jnp.int32)
    accum = jnp.zeros((SLOTS, RHS, W), jnp.float32)
    forward_levels = []
    for level in range(LEV):
        resid = (rhs[level].astype(jnp.float32) - accum).astype(jnp.bfloat16)
        forward = lax.map(rows_times, (resid, inv_diag[level])).astype(jnp.bfloat16)
        forward_levels.append(forward)
        if level < LEV - 1:
            update = lax.map(plain_times, (forward, coupling[level]))
            alive = column_ids[None, None, :] < counts[level][:, None, None]
            update = jnp.where(alive, update, 0.0).astype(jnp.bfloat16)
            target = (parents[level][:, None] * W + row_lists[level]).astype(jnp.int32)
            values = jnp.transpose(update, (0, 2, 1)).reshape(SLOTS * RU, RHS).astype(jnp.float32)
            flat = jnp.zeros((SLOTS * W, RHS), jnp.float32).at[target.reshape(-1)].add(values)
            accum = jnp.transpose(flat.reshape(SLOTS, W, RHS), (0, 2, 1))
    solved = [None] * LEV
    for level in reversed(range(LEV)):
        forward = forward_levels[level]
        if level == LEV - 1:
            reduced = forward
        else:
            upper = solved[level + 1]
            chosen = jnp.take(upper, parents[level], axis=0)
            picked = jnp.take_along_axis(chosen, row_lists[level][:, None, :], axis=2)
            alive = column_ids[None, None, :] < counts[level][:, None, None]
            picked = jnp.where(alive, picked, jnp.zeros((), picked.dtype))
            back_term = lax.map(rows_times, (picked, coupling[level]))
            reduced = (forward.astype(jnp.float32) - back_term).astype(jnp.bfloat16)
        solved[level] = lax.map(plain_times, (reduced, inv_diag[level])).astype(jnp.bfloat16)
    return jnp.stack(forward_levels), jnp.stack(solved)
```

```python
import functools

import jax
import jax.numpy as jnp
from jax import lax
from jax.experimental import pallas as pl
from jax.experimental.pallas import tpu as pltpu
from jax.sharding import Mesh, PartitionSpec as P

BF = jnp.bfloat16
F32 = jnp.float32
VMEM = pl.BlockSpec(memory_space=pltpu.VMEM)
SMEM = pl.BlockSpec(memory_space=pltpu.SMEM)
PARAMS = pltpu.CompilerParams(vmem_limit_bytes=32 * 1024 * 1024)
NT = (((1,), (1,)), ((), ()))
NN = (((1,), (0,)), ((), ()))


def mul_t(a, b):
    return lax.dot_general(a, b, NT, preferred_element_type=F32)


def mul(a, b):
    return lax.dot_general(a, b, NN, preferred_element_type=F32)


def call(body, outs, *args, specs=None, scratch=()):
    specs = [VMEM] * len(args) if specs is None else specs
    return pl.pallas_call(
        body,
        out_shape=outs,
        in_specs=specs,
        out_specs=jax.tree.map(lambda _: VMEM, outs),
        scratch_shapes=list(scratch),
        compiler_params=PARAMS,
    )(*args)


def sds(*shape, dtype=BF):
    return jax.ShapeDtypeStruct(shape, dtype)


def first_body(panels, info, r0, r1, r2, r3, inv, send, mine):
    p = info[2]
    quarter = r0.shape[-1]
    total = None
    for k, ref in enumerate((r0, r1, r2, r3)):
        q = lax.rem(p + panels - k, panels)
        block = ref[0, 0] if k == 0 else ref[...]
        part = mul_t(block, inv[:, pl.ds(pl.multiple_of(q * quarter, quarter), quarter)])
        total = part if total is None else total + part
    f = total.astype(BF)
    mine[...] = f
    rows = f.shape[0] // panels
    for d in range(panels):
        send[d, 0] = f[d * rows : (d + 1) * rows]
        send[d, 1] = r0[1, 0, d * rows : (d + 1) * rows]
        send[d, 2] = r0[2, 0, d * rows : (d + 1) * rows]


def place(lists, count, rows):
    cols = lists.shape[-1]
    row = lax.broadcasted_iota(jnp.int32, (rows, cols), 0)
    col = lax.broadcasted_iota(jnp.int32, (rows, cols), 1)
    return jnp.where((row == lists) & (col < count), 1.0, 0.0).astype(BF)


def updated(panels, p, f, lists, count, blocks, scratch):
    width = blocks[0].shape[-1]
    for k, ref in enumerate(blocks):
        q = lax.rem(p + panels - k, panels)
        scratch[:, pl.ds(pl.multiple_of(q * width, width), width)] = mul(f, ref[...]).astype(BF)
    u = scratch[...]
    col = lax.broadcasted_iota(jnp.int32, u.shape, 1)
    u = jnp.where(col < count, u.astype(F32), 0.0).astype(BF)
    return mul_t(u, place(lists, count, 4 * u.shape[1] // 2)).astype(BF)


def whole(ref, index):
    return jnp.concatenate([ref[q, index] for q in range(ref.shape[0])], axis=1)


def up0_body(panels, info, got, lists, c0, c1, c2, c3, out, scratch):
    f = whole(got, 0)
    e = updated(panels, info[2], f, lists[...], info[3], (c0, c1, c2, c3), scratch)
    for d in range(out.shape[0]):
        out[d] = e


def summed(recv):
    total = recv[0].astype(F32)
    for j in range(1, recv.shape[0]):
        total = total + recv[j].astype(F32)
    return total


def forward(resid, inv):
    return jnp.concatenate([mul_t(resid, inv[q]) for q in range(inv.shape[0])], axis=1).astype(BF)


def backward(reduced, inv):
    rows = inv.shape[1]
    total = None
    for q in range(inv.shape[0]):
        part = mul(reduced[:, q * rows : (q + 1) * rows], inv[q])
        total = part if total is None else total + part
    return total.astype(BF)


def up1_body(panels, info, recv, got, inv, lists, c0, c1, c2, c3, fout, out, scratch):
    resid = (whole(got, 1).astype(F32) - summed(recv)).astype(BF)
    f = forward(resid, inv)
    fout[...] = f
    e = updated(panels, info[2], f, lists[...], info[4], (c0, c1, c2, c3), scratch)
    for d in range(out.shape[0]):
        out[d] = e


def top_body(recv, got, inv, fout, out):
    resid = (whole(got, 2).astype(F32) - summed(recv)).astype(BF)
    f = forward(resid, inv)
    fout[...] = f
    s = backward(f, inv)
    for d in range(out.shape[0]):
        out[d] = s


def fold_body(slots, blocks, out, acc):
    acc[...] = jnp.zeros_like(acc)
    for j in range(blocks.shape[0]):
        d = slots[j]
        acc[d] = acc[d] + blocks[j].astype(F32)
    for d in range(out.shape[0]):
        out[d] = acc[d].astype(BF)


def route_body(slots, blocks, out):
    for d in range(out.shape[0]):
        out[d] = blocks[slots[d]]


def solved(panels, p, f, above, lists, count, blocks, inv, scratch):
    scratch[...] = mul(above, place(lists, count, above.shape[1])).astype(BF)
    width = blocks[0].shape[-1]
    back = None
    for k, ref in enumerate(blocks):
        q = lax.rem(p + panels - k, panels)
        term = mul_t(scratch[:, pl.ds(pl.multiple_of(q * width, width), width)], ref[...])
        back = term if back is None else back + term
    reduced = (f.astype(F32) - back).astype(BF)
    return backward(reduced, inv)


def down1_body(panels, info, recv, f, inv, lists, c0, c1, c2, c3, out, scratch):
    s = solved(panels, info[2], f[...], recv[info[6]], lists[...], info[4], (c0, c1, c2, c3), inv, scratch)
    for d in range(out.shape[0]):
        out[d] = s


def down0_body(panels, info, recv, got, inv, lists, c0, c1, c2, c3, f1, f2, s2, s1, send, scratch):
    s = solved(panels, info[2], whole(got, 0), recv[info[5]], lists[...], info[3], (c0, c1, c2, c3), inv, scratch)
    quarter = send.shape[-1]
    for index, value in enumerate((f1[...], f2[...], s2[0], s1[0], s)):
        for d in range(panels):
            send[d, index] = value[:, d * quarter : (d + 1) * quarter]


def last_body(panels, got, mine, fwd, sol):
    rows = got.shape[2]
    fwd[0, 0] = mine[...]
    for q in range(panels):
        span = slice(q * rows, (q + 1) * rows)
        fwd[1, 0, span] = got[q, 0]
        fwd[2, 0, span] = got[q, 1]
        sol[2, 0, span] = got[q, 2]
        sol[1, 0, span] = got[q, 3]
        sol[0, 0, span] = got[q, 4]


def local(sizes, rhs, inv_diag, coupling, row_lists, parents, counts):
    nz, group, panels = sizes
    leaf = lax.axis_index("z") * group + lax.axis_index("x") * 2 + lax.axis_index("core")
    z = leaf // group
    lane = leaf % group
    panel = lax.axis_index("panel")
    width = inv_diag.shape[3]
    mid = (group, rhs.shape[2] // panels, width)
    rows = rhs.shape[2] // panels

    def spread(x):
        return [x] + [
            lax.ppermute(x, "panel", [(i, (i + k) % panels) for i in range(panels)])
            for k in range(1, panels)
        ]

    mine0, mine1 = parents[0, leaf], parents[1, leaf]
    info = jnp.stack(
        [z, lane, panel, counts[0, leaf], counts[1, leaf], mine0 % group, mine1 % group]
    ).astype(jnp.int32)
    lists0 = lax.dynamic_slice_in_dim(row_lists[0], leaf, 1, 0)
    lists1 = lax.dynamic_slice_in_dim(row_lists[1], leaf, 1, 0)
    table = parents.reshape(2, nz, group)
    column = lax.dynamic_index_in_dim(table, lane, 2, keepdims=False)
    fold_slots = jnp.where(column // group == z, column % group, group).astype(jnp.int32)
    plane = lax.dynamic_index_in_dim(table, z, 1, keepdims=False)
    route_slots = (plane // group).astype(jnp.int32)

    rest = spread(rhs[0, 0])[1:]
    c0 = spread(coupling[0, 0])
    c1 = spread(coupling[1, 0])
    inv1 = lax.all_gather(inv_diag[1, 0], "panel", axis=0)
    inv2 = lax.all_gather(inv_diag[2, 0], "panel", axis=0)
    inv0 = lax.all_gather(inv_diag[0, 0], "panel", axis=0)

    send, mine = call(
        functools.partial(first_body, panels),
        (sds(panels, 3, rows, rhs.shape[3]), sds(rhs.shape[2], rhs.shape[3])),
        info, rhs, *rest, inv_diag[0, 0],
        specs=[SMEM] + [VMEM] * 5,
    )
    got = lax.all_to_all(send, "panel", 0, 0)
    touched = pltpu.VMEM((rows, panels * coupling.shape[3]), BF)
    e = call(
        functools.partial(up0_body, panels), sds(*mid), info, got, lists0, *c0,
        specs=[SMEM] + [VMEM] * 6, scratch=[touched],
    )

    def go_up(e, level):
        e = lax.all_to_all(e, "z", 0, 0)
        e = call(
            fold_body, sds(*mid), fold_slots[level], e,
            specs=[SMEM, VMEM], scratch=[pltpu.VMEM((group + 1, *mid[1:]), F32)],
        )
        return lax.all_to_all(e, ("x", "core"), 0, 0)

    def go_down(s, level):
        s = lax.all_to_all(s, "z", 0, 0)
        s = call(route_body, sds(*mid), route_slots[level], s, specs=[SMEM, VMEM])
        return lax.all_to_all(s, ("x", "core"), 0, 0)

    f1, e = call(
        functools.partial(up1_body, panels), (sds(*mid[1:]), sds(*mid)),
        info, go_up(e, 0), got, inv1, lists1, *c1,
        specs=[SMEM] + [VMEM] * 8, scratch=[touched],
    )
    f2, s2 = call(top_body, (sds(*mid[1:]), sds(*mid)), go_up(e, 1), got, inv2)
    s1 = call(
        functools.partial(down1_body, panels), sds(*mid),
        info, go_down(s2, 1), f1, inv1, lists1, *c1,
        specs=[SMEM] + [VMEM] * 8, scratch=[touched],
    )
    send = call(
        functools.partial(down0_body, panels), sds(panels, 5, rows, rhs.shape[3]),
        info, go_down(s1, 0), got, inv0, lists0, *c0, f1, f2, s2, s1,
        specs=[SMEM] + [VMEM] * 12, scratch=[touched],
    )
    got = lax.all_to_all(send, "panel", 0, 0)
    return call(
        functools.partial(last_body, panels), (sds(*rhs.shape), sds(*rhs.shape)), got, mine
    )


def solution(mesh):
    leaves, panels = mesh.shape["leaf"], mesh.shape["panel"]
    group = 8
    nz = leaves // group
    inner = Mesh(mesh.devices.reshape(nz, group // 2, 2, panels), ("z", "x", "core", "panel"))
    leaf = ("z", "x", "core")
    placed = (
        P(None, leaf, None, "panel"),
        P(None, leaf, "panel", None),
        P(None, leaf, None, "panel"),
        P(),
        P(),
        P(),
    )
    return jax.shard_map(
        functools.partial(local, (nz, group, panels)),
        mesh=inner,
        in_specs=placed,
        out_specs=(P(None, leaf, None, "panel"), P(None, leaf, None, "panel")),
        check_vma=False,
    )
```

```python
import functools

import jax
import jax.numpy as jnp
from jax import lax
from jax.experimental import pallas as pl
from jax.experimental.pallas import tpu as pltpu
from jax.sharding import Mesh, PartitionSpec as P

BF = jnp.bfloat16
F32 = jnp.float32
GROUP = 8
VMEM = pl.BlockSpec(memory_space=pltpu.VMEM)
SMEM = pl.BlockSpec(memory_space=pltpu.SMEM)
HBM = pl.BlockSpec(memory_space=pltpu.HBM)
PARAMS = pltpu.CompilerParams(vmem_limit_bytes=8 * 1024 * 1024)
NT = (((1,), (1,)), ((), ()))
NN = (((1,), (0,)), ((), ()))


def mul_t(a, b):
    return lax.dot_general(a, b, NT, preferred_element_type=F32)


def mul(a, b):
    return lax.dot_general(a, b, NN, preferred_element_type=F32)


def call(body, outs, *args, specs=None, outs_at=None, scratch=(), alias=None):
    specs = [VMEM] * len(args) if specs is None else specs
    outs = tuple(outs) if isinstance(outs, (list, tuple)) else outs
    outs_at = jax.tree.map(lambda _: VMEM, outs) if outs_at is None else tuple(outs_at)
    return pl.pallas_call(
        body,
        out_shape=outs,
        in_specs=specs,
        out_specs=outs_at,
        scratch_shapes=list(scratch),
        input_output_aliases=alias or {},
        compiler_params=PARAMS,
    )(*args)


def sds(*shape, dtype=BF):
    return jax.ShapeDtypeStruct(shape, dtype)


def leaf_place():
    z = lax.axis_index("z")
    lane = lax.axis_index("x") * lax.axis_size("core") + lax.axis_index("core")
    return z, lane, z * GROUP + lane


def order(k, panels):
    return lax.rem(lax.axis_index("panel") + panels - k, panels)


def pack_body(rhs, coupling, *outs):
    panels = len(outs) + 1
    quarter = rhs.shape[-1]
    for k, out in enumerate(outs, 1):
        target = lax.rem(lax.axis_index("panel") + k, panels)
        put_halves(out, rhs[0, 0])
        start = pl.multiple_of(target * quarter, quarter)
        out[2 * rhs.shape[2] :] = coupling[0, 0, pl.ds(start, quarter), :]


def put_halves(out, value):
    rows = value.shape[0]
    out[:rows] = value[:, :128]
    out[rows : 2 * rows] = value[:, 128:]


def first_body(rhs, coupling, m1, m2, m3, inv, send, mine, *cols):
    panels = send.shape[0]
    rows, quarter = rhs.shape[2:]
    total = None
    for k, ref in enumerate((rhs, m1, m2, m3)):
        q = order(k, panels)
        block = rhs[0, 0] if k == 0 else jnp.concatenate([ref[:rows], ref[rows : 2 * rows]], axis=1)
        part = mul_t(block, inv[:, pl.ds(pl.multiple_of(q * quarter, quarter), quarter)])
        total = part if total is None else total + part
    f = total.astype(BF)
    mine[...] = f
    few = rows // panels
    own = pl.multiple_of(lax.axis_index("panel") * quarter, quarter)
    for k, ref in enumerate((coupling, m1, m2, m3)):
        q = order(k, panels)
        part = mul(f, coupling[0, 0, pl.ds(own, quarter), :] if k == 0 else ref[2 * rows :])
        high = part.astype(BF)
        low = (part - high.astype(F32)).astype(BF)
        for d in range(panels):
            send[d, q] = high[d * few : (d + 1) * few]
            send[d, panels + q] = low[d * few : (d + 1) * few]
    for k, out in enumerate(cols):
        target = lax.rem(lax.axis_index("panel") + k, panels)
        out[...] = inv[:, pl.ds(pl.multiple_of(target * quarter, quarter), quarter)]
    for d in range(panels):
        span = slice(d * few, (d + 1) * few)
        for index, value in enumerate((f[span], rhs[1, 0, span], rhs[2, 0, span])):
            send[d, 2 * panels + 2 * index] = value[:, :128]
            send[d, 2 * panels + 2 * index + 1] = value[:, 128:]


def place_body(level, counts, lists, out):
    _, _, leaf = leaf_place()
    mine = lists[level, pl.ds(leaf, 1), :]
    row = lax.broadcasted_iota(jnp.int32, out.shape, 0)
    col = lax.broadcasted_iota(jnp.int32, out.shape, 1)
    out[...] = jnp.where((row == mine) & (col < counts[level, leaf]), 1.0, 0.0).astype(BF)


def laid_out(level, u, placed, counts):
    _, _, leaf = leaf_place()
    col = lax.broadcasted_iota(jnp.int32, u.shape, 1)
    u = jnp.where(col < counts[level, leaf], u, 0.0).astype(BF)
    return mul_t(u, placed[...]).astype(BF)


def whole(got, index):
    panels = got.shape[0]
    first = 2 * panels + 2 * index
    return jnp.concatenate(
        [got[q, first + half] for q in range(panels) for half in range(2)], axis=1
    )


def up0_body(counts, got, placed, out):
    panels = got.shape[0]
    pieces = []
    for q in range(panels):
        total = None
        for source in range(panels):
            part = got[source, q].astype(F32) + got[source, panels + q].astype(F32)
            total = part if total is None else total + part
        pieces.append(total)
    e = laid_out(0, jnp.concatenate(pieces, axis=1), placed, counts)
    for d in range(out.shape[0]):
        out[d] = e


def summed(recv):
    total = recv[0].astype(F32)
    for j in range(1, recv.shape[0]):
        total = total + recv[j].astype(F32)
    return total


def forward(resid, inv):
    return jnp.concatenate([mul_t(resid, inv[q]) for q in range(inv.shape[0])], axis=1).astype(BF)


def backward(reduced, inv):
    rows = inv.shape[1]
    total = None
    for q in range(inv.shape[0]):
        part = mul(reduced[:, q * rows : (q + 1) * rows], inv[q])
        total = part if total is None else total + part
    return total.astype(BF)


def to_all(out, value):
    for d in range(out.shape[0]):
        out[d] = value


def up1_body(counts, recv, got, inv, placed, c0, c1, c2, c3, fout, out, scratch):
    resid = (whole(got, 1).astype(F32) - summed(recv)).astype(BF)
    f = forward(resid, inv)
    fout[...] = f
    blocks = (c0, c1, c2, c3)
    width = c0.shape[-1]
    for k, ref in enumerate(blocks):
        q = order(k, len(blocks))
        scratch[:, pl.ds(pl.multiple_of(q * width, width), width)] = mul(f, ref[...])
    to_all(out, laid_out(1, scratch[...], placed, counts))


def top_body(recv, got, inv, fout, out):
    resid = (whole(got, 2).astype(F32) - summed(recv)).astype(BF)
    f = forward(resid, inv)
    fout[...] = f
    to_all(out, backward(f, inv))


def fold_body(level, parents, blocks, out, acc):
    z, lane, _ = leaf_place()
    acc[...] = jnp.zeros_like(acc)
    for j in range(blocks.shape[0]):
        parent = parents[level, j * GROUP + lane]
        d = jnp.where(lax.div(parent, GROUP) == z, lax.rem(parent, GROUP), GROUP)
        acc[d] = acc[d] + blocks[j].astype(F32)
    for d in range(out.shape[0]):
        out[d] = acc[d].astype(BF)


def route_body(level, parents, blocks, out):
    z, _, _ = leaf_place()
    for d in range(out.shape[0]):
        out[d] = blocks[lax.div(parents[level, z * GROUP + d], GROUP)]


def lessened(level, f, recv, parents, placed, blocks, scratch):
    _, _, leaf = leaf_place()
    above = recv[lax.rem(parents[level, leaf], GROUP)]
    scratch[...] = mul(above, placed[...]).astype(BF)
    width = blocks[0].shape[-1]
    back = None
    for k, ref in enumerate(blocks):
        q = order(k, len(blocks))
        term = mul_t(scratch[:, pl.ds(pl.multiple_of(q * width, width), width)], ref[...])
        back = term if back is None else back + term
    return (f.astype(F32) - back).astype(BF)


def down1_body(parents, recv, f, inv, placed, c0, c1, c2, c3, out, scratch):
    red = lessened(1, f[...], recv, parents, placed, (c0, c1, c2, c3), scratch)
    to_all(out, backward(red, inv))


def down0_body(parents, recv, got, placed, c0, c1, c2, c3, f1, f2, s2, s1, o0, o1, o2, o3, scratch):
    outs = (o0, o1, o2, o3)
    width = f1.shape[1]
    quarter = width // len(outs)
    red = lessened(0, whole(got, 0), recv, parents, placed, (c0, c1, c2, c3), scratch)
    for k, out in enumerate(outs):
        target = lax.rem(lax.axis_index("panel") + k, len(outs))
        cols = pl.ds(pl.multiple_of(target * quarter, quarter), quarter)
        out[:, :width] = red
        for index, value in enumerate((f1[:, cols], f2[:, cols], s2[0, :, cols], s1[0, :, cols])):
            out[:, width + index * quarter : width + (index + 1) * quarter] = value


def last_body(mine, *refs):
    panels = (len(refs) - 3) // 2
    ends, cols = refs[:panels], refs[panels : 2 * panels]
    fwd, sol, reds = refs[2 * panels :]
    width = reds.shape[1]
    quarter = width // panels
    rows = ends[0].shape[0]
    fwd[0, 0] = mine[...]
    for k in range(panels):
        q = order(k, panels)
        span = pl.ds(pl.multiple_of(q * rows, rows), rows)
        reds[span] = ends[k][:, :width]
        for index, (out, level) in enumerate(((fwd, 1), (fwd, 2), (sol, 2), (sol, 1))):
            out[level, 0, span] = ends[k][:, width + index * quarter : width + (index + 1) * quarter]
    total = None
    for k in range(panels):
        q = order(k, panels)
        part = mul(reds[:, pl.ds(pl.multiple_of(q * quarter, quarter), quarter)], cols[k][...])
        total = part if total is None else total + part
    sol[0, 0] = total.astype(BF)


def local(rhs, inv_diag, coupling, row_lists, parents, counts):
    panels = lax.axis_size("panel")
    rows = rhs.shape[2] // panels
    mid = (GROUP, rows, inv_diag.shape[3])
    after = lax.optimization_barrier

    def spread(x):
        return [x] + [
            lax.ppermute(x, "panel", [(i, (i + k) % panels) for i in range(panels)])
            for k in range(1, panels)
        ]

    def gathered(level):
        return lax.all_gather(inv_late[level, 0], "panel", axis=0)

    def shifted(x, k):
        return lax.ppermute(x, "panel", [(i, (i + k) % panels) for i in range(panels)])

    def placement(level, counts):
        return call(
            functools.partial(place_body, level),
            sds(inv_diag.shape[3], row_lists.shape[2]),
            counts, row_lists,
            specs=[SMEM, VMEM],
        )

    half = coupling.shape[3]
    tall = rhs.shape[3]
    packs = call(
        pack_body, [sds(2 * rhs.shape[2] + tall, half)] * (panels - 1), rhs, coupling,
    )
    packs = [shifted(x, k) for k, x in enumerate(packs, 1)]
    placed0 = placement(0, counts)
    inv1 = lax.all_gather(inv_diag[1, 0], "panel", axis=0)
    base = inv_diag[0, 0]
    in2, in3, in4 = inv_diag[2, 0], coupling[0, 0], coupling[1, 0]
    base, in2, in3, in4 = after((base, in2, in3, in4))
    send, mine, *cols = call(
        first_body,
        [sds(panels, 14, rows, half), sds(rhs.shape[2], tall)] + [sds(tall, tall)] * panels,
        rhs, coupling, *packs, base,
    )
    got = lax.all_to_all(send, "panel", 0, 0)
    touched = pltpu.VMEM((rows, panels * half), BF)
    wide = pltpu.VMEM((rows, panels * half), F32)
    e = call(up0_body, sds(*mid), counts, got, placed0, specs=[SMEM] + [VMEM] * 2)
    e, early, in2, in4 = after((e, counts, in2, in4))
    c1 = spread(in4)
    inv2 = lax.all_gather(in2, "panel", axis=0)

    def beside(x, axes, small):
        x, small = after((x, small))
        x = lax.all_to_all(x, axes, 0, 0)
        return after((x, jnp.maximum(small, 0)))

    def fold(e, level, table):
        return call(
            functools.partial(fold_body, level), sds(*mid), table, e,
            specs=[SMEM, VMEM], scratch=[pltpu.VMEM((GROUP + 1, *mid[1:]), F32)],
        )

    def route(s, level, table):
        return call(functools.partial(route_body, level), sds(*mid), table, s, specs=[SMEM, VMEM])

    e = lax.all_to_all(e, "z", 0, 0)
    e, placed1 = after((e, placement(1, early)))
    e = fold(e, 0, parents)
    e = lax.all_to_all(e, ("x", "core"), 0, 0)
    f1, e = call(
        up1_body, (sds(*mid[1:]), sds(*mid)),
        counts, e, got, inv1, placed1, *c1,
        specs=[SMEM] + [VMEM] * 8, scratch=[wide],
    )
    e, table = beside(e, "z", parents)
    e = fold(e, 1, table)
    e = lax.all_to_all(e, ("x", "core"), 0, 0)
    f2, s2 = call(top_body, (sds(*mid[1:]), sds(*mid)), e, got, inv2)
    s = lax.all_to_all(s2, "z", 0, 0)
    s = route(s, 1, table)
    s = lax.all_to_all(s, ("x", "core"), 0, 0)
    s1 = call(
        down1_body, sds(*mid),
        table, s, f1, inv1, placed1, *c1,
        specs=[SMEM] + [VMEM] * 8, scratch=[touched],
    )
    s, in3, *cols = after((s1, in3, *cols))
    c0 = spread(in3)
    cols = cols[:1] + [shifted(x, k) for k, x in enumerate(cols[1:], 1)]
    s = lax.all_to_all(s, "z", 0, 0)
    s = route(s, 0, table)
    s = lax.all_to_all(s, ("x", "core"), 0, 0)
    ends = call(
        down0_body, [sds(rows, 2 * mid[2])] * panels,
        table, s, got, placed0, *c0, f1, f2, s2, s1,
        specs=[SMEM] + [VMEM] * 11, scratch=[touched],
    )
    ends = [ends[0]] + [shifted(x, k) for k, x in enumerate(ends[1:], 1)]
    return call(
        last_body, (sds(*rhs.shape), sds(*rhs.shape)), mine, *ends, *cols,
        scratch=[pltpu.VMEM((rhs.shape[2], mid[2]), BF)],
    )


def solution(mesh):
    leaves, panels = mesh.shape["leaf"], mesh.shape["panel"]
    inner = Mesh(
        mesh.devices.reshape(leaves // GROUP, GROUP // 2, 2, panels), ("z", "x", "core", "panel")
    )
    leaf = ("z", "x", "core")
    placed = (
        P(None, leaf, None, "panel"),
        P(None, leaf, "panel", None),
        P(None, leaf, None, "panel"),
        P(),
        P(),
        P(),
    )
    return jax.shard_map(
        local,
        mesh=inner,
        in_specs=placed,
        out_specs=(P(None, leaf, None, "panel"), P(None, leaf, None, "panel")),
        check_vma=False,
    )
```

```python
import functools

import jax
import jax.numpy as jnp
from jax import lax
from jax.experimental import pallas as pl
from jax.experimental.pallas import tpu as pltpu
from jax.sharding import Mesh, PartitionSpec as P

BF = jnp.bfloat16
F32 = jnp.float32
GROUP = 8
VMEM = pl.BlockSpec(memory_space=pltpu.VMEM)
SMEM = pl.BlockSpec(memory_space=pltpu.SMEM)
HBM = pl.BlockSpec(memory_space=pltpu.HBM)
PARAMS = pltpu.CompilerParams(vmem_limit_bytes=8 * 1024 * 1024)
NT = (((1,), (1,)), ((), ()))
NN = (((1,), (0,)), ((), ()))


def mul_t(a, b):
    return lax.dot_general(a, b, NT, preferred_element_type=F32)


def mul(a, b):
    return lax.dot_general(a, b, NN, preferred_element_type=F32)


def call(body, outs, *args, specs=None, outs_at=VMEM, scratch=()):
    specs = [VMEM] * len(args) if specs is None else specs
    args = [far(x) if spec is HBM else x for x, spec in zip(args, specs)]
    return pl.pallas_call(
        body,
        out_shape=tuple(outs) if isinstance(outs, list) else outs,
        in_specs=specs,
        out_specs=outs_at if isinstance(outs_at, list) else jax.tree.map(lambda _: outs_at, outs),
        scratch_shapes=list(scratch),
        compiler_params=PARAMS,
    )(*args)


def far(x):
    return pltpu.with_memory_space_constraint(x, pltpu.HBM)


def sds(*shape, dtype=BF):
    return jax.ShapeDtypeStruct(shape, dtype)


def leaf_place():
    z = lax.axis_index("z")
    lane = lax.axis_index("x") * lax.axis_size("core") + lax.axis_index("core")
    return z, lane, z * GROUP + lane


def order(k, panels):
    return lax.rem(lax.axis_index("panel") + panels - k, panels)


def pack_body(rhs, coupling, *outs):
    panels = len(outs) + 1
    quarter = rhs.shape[-1]
    for k, out in enumerate(outs, 1):
        target = lax.rem(lax.axis_index("panel") + k, panels)
        put_halves(out, rhs[0, 0])
        start = pl.multiple_of(target * quarter, quarter)
        out[2 * rhs.shape[2] :] = coupling[0, 0, pl.ds(start, quarter), :]


def fold_coupling_body(coupling, out):
    width = coupling.shape[-1]
    rows = out.shape[0]
    for part in range(out.shape[1] // width):
        out[:, part * width : (part + 1) * width] = coupling[
            1, 0, part * rows : (part + 1) * rows, :
        ]


def last_weights_body(coupling, inv, *refs):
    *outs, sems = refs
    rows = inv.shape[2]
    width = coupling.shape[-1]
    parts = len(outs)
    copies = []
    for k, out in enumerate(outs):
        target = lax.rem(lax.axis_index("panel") + k, parts)
        for part in range(parts):
            source = coupling.at[0, 0, pl.ds(part * rows, rows)]
            copies.append((source, out.at[:, pl.ds(part * width, width)]))
        cols = pl.ds(pl.multiple_of(target * rows, rows), rows)
        copies.append((inv.at[0, 0, :, cols], out.at[:, pl.ds(parts * width, rows)]))
    copies = [pltpu.make_async_copy(a, b, sems.at[i]) for i, (a, b) in enumerate(copies)]
    for copy in copies:
        copy.start()
    for copy in copies:
        copy.wait()


def put_halves(out, value):
    rows = value.shape[0]
    out[:rows] = value[:, :128]
    out[rows : 2 * rows] = value[:, 128:]


def first_body(rhs, coupling, m1, m2, m3, inv, send):
    panels = send.shape[0]
    rows, quarter = rhs.shape[2:]
    total = None
    for k, ref in enumerate((rhs, m1, m2, m3)):
        q = order(k, panels)
        block = rhs[0, 0] if k == 0 else jnp.concatenate([ref[:rows], ref[rows : 2 * rows]], axis=1)
        part = mul_t(block, inv[:, pl.ds(pl.multiple_of(q * quarter, quarter), quarter)])
        total = part if total is None else total + part
    f = total.astype(BF)
    few = rows // panels
    own = pl.multiple_of(lax.axis_index("panel") * quarter, quarter)
    for k, ref in enumerate((coupling, m1, m2, m3)):
        q = order(k, panels)
        part = mul(f, coupling[0, 0, pl.ds(own, quarter), :] if k == 0 else ref[2 * rows :])
        high = part.astype(BF)
        low = (part - high.astype(F32)).astype(BF)
        for d in range(panels):
            send[d, q] = high[d * few : (d + 1) * few]
            send[d, panels + q] = low[d * few : (d + 1) * few]
    for d in range(panels):
        span = slice(d * few, (d + 1) * few)
        for index, value in enumerate((f[span], rhs[1, 0, span], rhs[2, 0, span])):
            send[d, 2 * panels + 2 * index] = value[:, :128]
            send[d, 2 * panels + 2 * index + 1] = value[:, 128:]


def place(level, counts, lists, rows):
    _, _, leaf = leaf_place()
    mine = lists[level, pl.ds(leaf, 1), :]
    shape = (rows, lists.shape[-1])
    row = lax.broadcasted_iota(jnp.int32, shape, 0)
    col = lax.broadcasted_iota(jnp.int32, shape, 1)
    return jnp.where((row == mine) & (col < counts[level, leaf]), 1.0, 0.0).astype(BF)


def place_body(level, counts, lists, out):
    out[...] = place(level, counts, lists, out.shape[0])


def laid_out(level, u, placed, counts):
    _, _, leaf = leaf_place()
    col = lax.broadcasted_iota(jnp.int32, u.shape, 1)
    u = jnp.where(col < counts[level, leaf], u, 0.0).astype(BF)
    return mul_t(u, placed).astype(BF)


def whole(got, index):
    panels = got.shape[0]
    first = 2 * panels + 2 * index
    return jnp.concatenate(
        [got[q, first + half] for q in range(panels) for half in range(2)], axis=1
    )


def up0_body(counts, got, placed, out):
    panels = got.shape[0]
    pieces = []
    for q in range(panels):
        total = None
        for source in range(panels):
            part = got[source, q].astype(F32) + got[source, panels + q].astype(F32)
            total = part if total is None else total + part
        pieces.append(total)
    e = laid_out(0, jnp.concatenate(pieces, axis=1), placed[...], counts)
    for d in range(out.shape[0]):
        out[d] = e


def summed(recv):
    total = recv[0].astype(F32)
    for j in range(1, recv.shape[0]):
        total = total + recv[j].astype(F32)
    return total


def forward(resid, blocks, out):
    rows, cols = blocks[0].shape[0], out.shape[1]
    for k, ref in enumerate(blocks):
        start = pl.multiple_of(order(k, len(blocks)) * rows, rows)
        out[:, pl.ds(start, rows)] = mul_t(resid, ref[:, :cols]).astype(BF)
    return out[...]


def backward(reduced, blocks):
    rows, cols = blocks[0].shape[0], reduced.shape[1]
    total = None
    for k, ref in enumerate(blocks):
        start = pl.multiple_of(order(k, len(blocks)) * rows, rows)
        part = mul(reduced[:, pl.ds(start, rows)], ref[:, :cols])
        total = part if total is None else total + part
    return total.astype(BF)


def coupled(f, blocks, first, out):
    rows = blocks[0].shape[0]
    parts = f.shape[1] // rows
    width = out.shape[1] // len(blocks)
    for k, ref in enumerate(blocks):
        total = None
        for part in range(parts):
            lanes = slice(first + part * width, first + (part + 1) * width)
            term = mul(f[:, part * rows : (part + 1) * rows], ref[:, lanes])
            total = term if total is None else total + term
        out[:, pl.ds(pl.multiple_of(order(k, len(blocks)) * width, width), width)] = total


def lessened(level, f, recv, parents, placed, blocks, first, picked):
    _, _, leaf = leaf_place()
    above = recv[lax.rem(parents[level, leaf], GROUP)]
    picked[...] = mul(above, placed).astype(BF)
    rows = blocks[0].shape[0]
    width = picked.shape[1] // len(blocks)
    pieces = []
    for part in range(f.shape[1] // rows):
        lanes = slice(first + part * width, first + (part + 1) * width)
        total = None
        for k, ref in enumerate(blocks):
            start = pl.multiple_of(order(k, len(blocks)) * width, width)
            term = mul_t(picked[:, pl.ds(start, width)], ref[:, lanes])
            total = term if total is None else total + term
        pieces.append(total)
    return (f.astype(F32) - jnp.concatenate(pieces, axis=1)).astype(BF)


def to_all(out, value):
    for d in range(out.shape[0]):
        out[d] = value


def up1_body(counts, recv, got, lists, i0, i1, i2, i3, c0, c1, c2, c3, fout, out, keep, scratch, sems):
    inverse, blocks = (i0, i1, i2, i3), (c0, c1, c2, c3)
    cols = i0.shape[1]
    copies = []
    for k in range(len(blocks)):
        for part, (source, span) in enumerate(
            ((inverse[k], pl.ds(0, cols)), (blocks[k], pl.ds(cols, c0.shape[1])))
        ):
            copies.append(pltpu.make_async_copy(source, keep.at[k, :, span], sems.at[k, part]))
    for copy in copies:
        copy.start()
    resid = (whole(got, 1).astype(F32) - summed(recv)).astype(BF)
    placed = place(1, counts, lists, fout.shape[1])
    f = forward(resid, inverse, fout)
    coupled(f, blocks, 0, scratch)
    to_all(out, laid_out(1, scratch[...], placed, counts))
    for copy in copies:
        copy.wait()


def top_body(recv, got, i0, i1, i2, i3, fout, out):
    resid = (whole(got, 2).astype(F32) - summed(recv)).astype(BF)
    blocks = (i0, i1, i2, i3)
    forward(resid, blocks, fout)
    to_all(out, backward(fout, blocks))


def fold_body(level, parents, blocks, out, acc):
    z, lane, _ = leaf_place()
    acc[...] = jnp.zeros_like(acc)
    for j in range(blocks.shape[0]):
        parent = parents[level, j * GROUP + lane]
        d = jnp.where(lax.div(parent, GROUP) == z, lax.rem(parent, GROUP), GROUP)
        acc[d] = acc[d] + blocks[j].astype(F32)
    for d in range(out.shape[0]):
        out[d] = acc[d].astype(BF)


def route_body(level, parents, blocks, out):
    z, _, _ = leaf_place()
    for d in range(out.shape[0]):
        out[d] = blocks[lax.div(parents[level, z * GROUP + d], GROUP)]


def down1_body(parents, counts, recv, f, lists, keep, out, picked, red):
    blocks = [keep.at[k] for k in range(keep.shape[0])]
    placed = place(1, counts, lists, red.shape[1])
    red[...] = lessened(1, f[...], recv, parents, placed, blocks, red.shape[1], picked)
    to_all(out, backward(red, blocks))


def down0_body(
    parents, counts, recv, got, lists, b0, b1, b2, b3, f1, f2, s2, s1,
    o0, o1, o2, o3, scratch, f0,
):
    outs = (o0, o1, o2, o3)
    width = f1.shape[1]
    quarter = width // len(outs)
    f0[...] = whole(got, 0)
    placed = place(0, counts, lists, width)
    red = lessened(0, f0[...], recv, parents, placed, (b0, b1, b2, b3), 0, scratch)
    for k, out in enumerate(outs):
        target = lax.rem(lax.axis_index("panel") + k, len(outs))
        cols = pl.ds(pl.multiple_of(target * quarter, quarter), quarter)
        out[:, :width] = red
        for index, value in enumerate(
            (f0[:, cols], f1[:, cols], f2[:, cols], s2[0, :, cols], s1[0, :, cols])
        ):
            out[:, width + index * quarter : width + (index + 1) * quarter] = value


def last_body(*refs):
    panels = (len(refs) - 3) // 2
    ends, cols = refs[:panels], refs[panels : 2 * panels]
    fwd, sol, reds = refs[2 * panels :]
    width = reds.shape[1]
    quarter = width // panels
    rows = ends[0].shape[0]
    for k in range(panels):
        q = order(k, panels)
        span = pl.ds(pl.multiple_of(q * rows, rows), rows)
        reds[span] = ends[k][:, :width]
        for index, (out, level) in enumerate(
            ((fwd, 0), (fwd, 1), (fwd, 2), (sol, 2), (sol, 1))
        ):
            out[level, 0, span] = ends[k][:, width + index * quarter : width + (index + 1) * quarter]
    total = None
    for k in range(panels):
        q = order(k, panels)
        part = mul(
            reds[:, pl.ds(pl.multiple_of(q * quarter, quarter), quarter)], cols[k][:, -quarter:]
        )
        total = part if total is None else total + part
    sol[0, 0] = total.astype(BF)


def local(rhs, inv_diag, coupling, row_lists, parents, counts):
    panels = lax.axis_size("panel")
    rows = rhs.shape[2] // panels
    mid = (GROUP, rows, inv_diag.shape[3])
    after = lax.optimization_barrier

    def shifted(x, k):
        return lax.ppermute(x, "panel", [(i, (i + k) % panels) for i in range(panels)])

    def placement(level, counts):
        return call(
            functools.partial(place_body, level),
            sds(inv_diag.shape[3], row_lists.shape[2]),
            counts, row_lists,
            specs=[SMEM, VMEM],
        )

    half = coupling.shape[3]
    tall = rhs.shape[3]
    half = coupling.shape[3]
    tall = rhs.shape[3]
    width = inv_diag.shape[3]

    def exchange(x, axes, weights=(), shifts=()):
        x, *weights = after((x, *weights))
        moved = [shifted(w, k) for w, k in zip(weights, shifts)]
        x = lax.all_to_all(x, axes, 0, 0)
        return after((x, *moved))

    packs = call(
        pack_body, [sds(2 * rhs.shape[2] + tall, half)] * (panels - 1), rhs, coupling,
    )
    packs = [shifted(x, k) for k, x in enumerate(packs, 1)]
    base = inv_diag[0, 0]
    placed0 = placement(0, counts)
    c1 = call(fold_coupling_body, sds(tall, panels * half), coupling)
    in1, in2 = inv_diag[1, 0], inv_diag[2, 0]
    base, placed0, c1, in1, in2 = after((base, placed0, c1, in1, in2))
    send = call(
        first_body, sds(panels, 14, rows, half), rhs, coupling, *packs, base,
    )
    got, c11, c13 = exchange(send, "panel", [c1, c1], [1, 3])
    touched = pltpu.VMEM((rows, panels * half), BF)
    wide = pltpu.VMEM((rows, panels * half), F32)
    e = call(up0_body, sds(*mid), counts, got, placed0, specs=[SMEM] + [VMEM] * 2)

    def fold(e, level, table):
        return call(
            functools.partial(fold_body, level), sds(*mid), table, e,
            specs=[SMEM, VMEM], scratch=[pltpu.VMEM((GROUP + 1, *mid[1:]), F32)],
        )

    def route(s, level, table):
        return call(functools.partial(route_body, level), sds(*mid), table, s, specs=[SMEM, VMEM])

    e, in11, in13, c12 = exchange(e, "z", [in1, in1, c1], [1, 3, 2])
    e = fold(e, 0, parents)
    e, in12 = exchange(e, ("x", "core"), [in1], [2])
    level1 = (in1, in11, in12, in13, c1, c11, c12, c13)
    f1, e, keep = call(
        up1_body, [sds(*mid[1:]), sds(*mid), sds(panels, tall, width + panels * half)],
        counts, e, got, row_lists, *level1,
        specs=[SMEM] + [VMEM] * 11, outs_at=[VMEM, VMEM, HBM],
        scratch=[wide, pltpu.SemaphoreType.DMA((panels, 2))],
    )
    e, in21, in23 = exchange(e, "z", [in2, in2], [1, 3])
    e = fold(e, 1, parents)
    e, in22 = exchange(e, ("x", "core"), [in2], [2])
    f2, s2 = call(
        top_body, (sds(*mid[1:]), sds(*mid)), e, got, in2, in21, in22, in23
    )
    s, inv_late, near_coupling = after((s2, inv_diag, coupling))
    w0 = call(
        last_weights_body, [sds(tall, panels * half + tall)] * panels, near_coupling, inv_late,
        specs=[HBM] * 2, outs_at=HBM,
        scratch=[pltpu.SemaphoreType.DMA((panels * (panels + 1),))],
    )
    s = lax.all_to_all(s, "z", 0, 0)
    s, *w0 = after((s, *w0))
    s = route(s, 1, parents)
    s, w01, w03 = exchange(s, ("x", "core"), [w0[1], w0[3]], [1, 3])
    s1 = call(
        down1_body, sds(*mid), parents, counts, s, f1, row_lists, keep,
        specs=[SMEM] * 2 + [VMEM] * 4, scratch=[touched, pltpu.VMEM(mid[1:], BF)],
    )
    s, far2 = after((s1, w0[2]))
    w02 = shifted(far2, 2)
    s = lax.all_to_all(s, "z", 0, 0)
    w0 = (w0[0], w01, w02, w03)
    s = route(s, 0, parents)
    s = lax.all_to_all(s, ("x", "core"), 0, 0)
    ends = call(
        down0_body, [sds(rows, mid[2] + 5 * tall)] * panels,
        parents, counts, s, got, row_lists, *w0, f1, f2, s2, s1,
        specs=[SMEM] * 2 + [VMEM] * 11, scratch=[touched, pltpu.VMEM(mid[1:], BF)],
    )
    ends = [ends[0]] + [shifted(x, k) for k, x in enumerate(ends[1:], 1)]
    return call(
        last_body, (sds(*rhs.shape), sds(*rhs.shape)), *ends, *w0,
        scratch=[pltpu.VMEM((rhs.shape[2], mid[2]), BF)],
    )


def solution(mesh):
    leaves, panels = mesh.shape["leaf"], mesh.shape["panel"]
    inner = Mesh(
        mesh.devices.reshape(leaves // GROUP, GROUP // 2, 2, panels), ("z", "x", "core", "panel")
    )
    leaf = ("z", "x", "core")
    placed = (
        P(None, leaf, None, "panel"),
        P(None, leaf, "panel", None),
        P(None, leaf, None, "panel"),
        P(),
        P(),
        P(),
    )
    return jax.shard_map(
        local,
        mesh=inner,
        in_specs=placed,
        out_specs=(P(None, leaf, None, "panel"), P(None, leaf, None, "panel")),
        check_vma=False,
    )
```

```python
import functools

import jax
import jax.numpy as jnp
from jax import lax
from jax.experimental import pallas as pl
from jax.experimental.pallas import tpu as pltpu
from jax.sharding import Mesh, PartitionSpec as P

BF = jnp.bfloat16
F32 = jnp.float32
GROUP = 8
VMEM = pl.BlockSpec(memory_space=pltpu.VMEM)
SMEM = pl.BlockSpec(memory_space=pltpu.SMEM)
HBM = pl.BlockSpec(memory_space=pltpu.HBM)
PARAMS = pltpu.CompilerParams(vmem_limit_bytes=8 * 1024 * 1024)
NT = (((1,), (1,)), ((), ()))
NN = (((1,), (0,)), ((), ()))


def mul_t(a, b):
    return lax.dot_general(a, b, NT, preferred_element_type=F32)


def mul(a, b):
    return lax.dot_general(a, b, NN, preferred_element_type=F32)


def call(body, outs, *args, specs=None, outs_at=VMEM, scratch=()):
    specs = [VMEM] * len(args) if specs is None else specs
    args = [far(x) if spec is HBM else x for x, spec in zip(args, specs)]
    return pl.pallas_call(
        body,
        out_shape=tuple(outs) if isinstance(outs, list) else outs,
        in_specs=specs,
        out_specs=outs_at if isinstance(outs_at, list) else jax.tree.map(lambda _: outs_at, outs),
        scratch_shapes=list(scratch),
        compiler_params=PARAMS,
    )(*args)


def far(x):
    return pltpu.with_memory_space_constraint(x, pltpu.HBM)


def sds(*shape, dtype=BF):
    return jax.ShapeDtypeStruct(shape, dtype)


def leaf_place():
    z = lax.axis_index("z")
    lane = lax.axis_index("x") * lax.axis_size("core") + lax.axis_index("core")
    return z, lane, z * GROUP + lane


def order(k, panels):
    return lax.rem(lax.axis_index("panel") + panels - k, panels)


def pack_body(rhs, coupling, own, beside, *refs):
    *outs, sems = refs
    panels = len(outs) + 1
    rows, quarter = rhs.shape[2:]
    width = coupling.shape[-1]
    pairs = []
    for k, out in enumerate((own, *outs)):
        target = lax.rem(lax.axis_index("panel") + k, panels)
        start = pl.multiple_of(target * quarter, quarter)
        source = coupling.at[0, 0, pl.ds(start, quarter)]
        if k == 0:
            pairs.append((source, out))
            continue
        pairs.append((source, out.at[pl.ds(2 * rows, quarter)]))
        for half in range(2):
            lanes = pl.ds(half * width, width)
            pairs.append((rhs.at[0, 0, :, lanes], out.at[pl.ds(half * rows, rows)]))
    for part in range(panels):
        source = coupling.at[1, 0, pl.ds(part * quarter, quarter)]
        pairs.append((source, beside.at[:, pl.ds(part * width, width)]))
    copies = [pltpu.make_async_copy(a, b, sems.at[i]) for i, (a, b) in enumerate(pairs)]
    for copy in copies:
        copy.start()
    for copy in copies:
        copy.wait()


def last_weights_body(coupling, inv, *refs):
    *outs, sems = refs
    rows = inv.shape[2]
    width = coupling.shape[-1]
    parts = len(outs)
    copies = []
    for k, out in enumerate(outs):
        target = lax.rem(lax.axis_index("panel") + k, parts)
        for part in range(parts):
            source = coupling.at[0, 0, pl.ds(part * rows, rows)]
            copies.append((source, out.at[:, pl.ds(part * width, width)]))
        cols = pl.ds(pl.multiple_of(target * rows, rows), rows)
        copies.append((inv.at[0, 0, :, cols], out.at[:, pl.ds(parts * width, rows)]))
    copies = [pltpu.make_async_copy(a, b, sems.at[i]) for i, (a, b) in enumerate(copies)]
    for copy in copies:
        copy.start()
    for copy in copies:
        copy.wait()


def first_body(rhs, own, m1, m2, m3, inv, send):
    panels = send.shape[0]
    rows, quarter = rhs.shape[2:]
    total = None
    for k, ref in enumerate((rhs, m1, m2, m3)):
        q = order(k, panels)
        block = rhs[0, 0] if k == 0 else jnp.concatenate([ref[:rows], ref[rows : 2 * rows]], axis=1)
        part = mul_t(block, inv[:, pl.ds(pl.multiple_of(q * quarter, quarter), quarter)])
        total = part if total is None else total + part
    f = total.astype(BF)
    few = rows // panels
    for k, ref in enumerate((own, m1, m2, m3)):
        q = order(k, panels)
        part = mul(f, own[...] if k == 0 else ref[2 * rows :])
        high = part.astype(BF)
        low = (part - high.astype(F32)).astype(BF)
        for d in range(panels):
            send[d, q] = high[d * few : (d + 1) * few]
            send[d, panels + q] = low[d * few : (d + 1) * few]
    for d in range(panels):
        span = slice(d * few, (d + 1) * few)
        for index, value in enumerate((f[span], rhs[1, 0, span], rhs[2, 0, span])):
            send[d, 2 * panels + 2 * index] = value[:, :128]
            send[d, 2 * panels + 2 * index + 1] = value[:, 128:]


def place(level, counts, lists, rows):
    _, _, leaf = leaf_place()
    mine = lists[level, pl.ds(leaf, 1), :]
    shape = (rows, lists.shape[-1])
    row = lax.broadcasted_iota(jnp.int32, shape, 0)
    col = lax.broadcasted_iota(jnp.int32, shape, 1)
    return jnp.where((row == mine) & (col < counts[level, leaf]), 1.0, 0.0).astype(BF)


def place_body(level, counts, lists, out):
    out[...] = place(level, counts, lists, out.shape[0])


def laid_out(level, u, placed, counts):
    _, _, leaf = leaf_place()
    col = lax.broadcasted_iota(jnp.int32, u.shape, 1)
    u = jnp.where(col < counts[level, leaf], u, 0.0).astype(BF)
    return mul_t(u, placed).astype(BF)


def whole(got, index):
    panels = got.shape[0]
    first = 2 * panels + 2 * index
    return jnp.concatenate(
        [got[q, first + half] for q in range(panels) for half in range(2)], axis=1
    )


def up0_body(counts, got, placed, out):
    panels = got.shape[0]
    pieces = []
    for q in range(panels):
        total = None
        for source in range(panels):
            part = got[source, q].astype(F32) + got[source, panels + q].astype(F32)
            total = part if total is None else total + part
        pieces.append(total)
    e = laid_out(0, jnp.concatenate(pieces, axis=1), placed[...], counts)
    for d in range(out.shape[0]):
        out[d] = e


def summed(recv):
    total = recv[0].astype(F32)
    for j in range(1, recv.shape[0]):
        total = total + recv[j].astype(F32)
    return total


def forward(resid, blocks, out):
    rows, cols = blocks[0].shape[0], out.shape[1]
    for k, ref in enumerate(blocks):
        start = pl.multiple_of(order(k, len(blocks)) * rows, rows)
        out[:, pl.ds(start, rows)] = mul_t(resid, ref[:, :cols]).astype(BF)
    return out[...]


def backward(reduced, blocks):
    rows, cols = blocks[0].shape[0], reduced.shape[1]
    total = None
    for k, ref in enumerate(blocks):
        start = pl.multiple_of(order(k, len(blocks)) * rows, rows)
        part = mul(reduced[:, pl.ds(start, rows)], ref[:, :cols])
        total = part if total is None else total + part
    return total.astype(BF)


def coupled(f, blocks, first, out):
    rows = blocks[0].shape[0]
    parts = f.shape[1] // rows
    width = out.shape[1] // len(blocks)
    for k, ref in enumerate(blocks):
        total = None
        for part in range(parts):
            lanes = slice(first + part * width, first + (part + 1) * width)
            term = mul(f[:, part * rows : (part + 1) * rows], ref[:, lanes])
            total = term if total is None else total + term
        out[:, pl.ds(pl.multiple_of(order(k, len(blocks)) * width, width), width)] = total


def lessened(level, f, recv, parents, placed, blocks, first, picked):
    _, _, leaf = leaf_place()
    above = recv[lax.rem(parents[level, leaf], GROUP)]
    picked[...] = mul(above, placed).astype(BF)
    rows = blocks[0].shape[0]
    width = picked.shape[1] // len(blocks)
    pieces = []
    for part in range(f.shape[1] // rows):
        lanes = slice(first + part * width, first + (part + 1) * width)
        total = None
        for k, ref in enumerate(blocks):
            start = pl.multiple_of(order(k, len(blocks)) * width, width)
            term = mul_t(picked[:, pl.ds(start, width)], ref[:, lanes])
            total = term if total is None else total + term
        pieces.append(total)
    return (f.astype(F32) - jnp.concatenate(pieces, axis=1)).astype(BF)


def to_all(out, value):
    for d in range(out.shape[0]):
        out[d] = value


def up1_body(counts, recv, got, lists, i0, i1, i2, i3, c0, c1, c2, c3, fout, out, keep, scratch, sems):
    inverse, blocks = (i0, i1, i2, i3), (c0, c1, c2, c3)
    cols = i0.shape[1]
    copies = []
    for k in range(len(blocks)):
        for part, (source, span) in enumerate(
            ((inverse[k], pl.ds(0, cols)), (blocks[k], pl.ds(cols, c0.shape[1])))
        ):
            copies.append(pltpu.make_async_copy(source, keep.at[k, :, span], sems.at[k, part]))
    for copy in copies:
        copy.start()
    resid = (whole(got, 1).astype(F32) - summed(recv)).astype(BF)
    placed = place(1, counts, lists, fout.shape[1])
    f = forward(resid, inverse, fout)
    coupled(f, blocks, 0, scratch)
    to_all(out, laid_out(1, scratch[...], placed, counts))
    for copy in copies:
        copy.wait()


def top_body(recv, got, i0, i1, i2, i3, fout, out):
    resid = (whole(got, 2).astype(F32) - summed(recv)).astype(BF)
    blocks = (i0, i1, i2, i3)
    forward(resid, blocks, fout)
    to_all(out, backward(fout, blocks))


def fold_body(level, parents, blocks, out, acc):
    z, lane, _ = leaf_place()
    acc[...] = jnp.zeros_like(acc)
    for j in range(blocks.shape[0]):
        parent = parents[level, j * GROUP + lane]
        d = jnp.where(lax.div(parent, GROUP) == z, lax.rem(parent, GROUP), GROUP)
        acc[d] = acc[d] + blocks[j].astype(F32)
    for d in range(out.shape[0]):
        out[d] = acc[d].astype(BF)


def route_body(level, parents, blocks, out):
    z, _, _ = leaf_place()
    for d in range(out.shape[0]):
        out[d] = blocks[lax.div(parents[level, z * GROUP + d], GROUP)]


def down1_body(parents, counts, recv, f, lists, keep, out, picked, red, held, sems):
    cols = red.shape[1]
    parts = (pl.ds(cols, held.shape[2] - cols), pl.ds(0, cols))
    copies = [
        [
            pltpu.make_async_copy(keep.at[k, :, span], held.at[k, :, span], sems.at[k, part])
            for k in range(keep.shape[0])
        ]
        for part, span in enumerate(parts)
    ]
    for copy in copies[0] + copies[1]:
        copy.start()
    blocks = [held.at[k] for k in range(keep.shape[0])]
    placed = place(1, counts, lists, cols)
    for copy in copies[0]:
        copy.wait()
    red[...] = lessened(1, f[...], recv, parents, placed, blocks, cols, picked)
    for copy in copies[1]:
        copy.wait()
    to_all(out, backward(red, blocks))


def down0_body(
    parents, counts, recv, got, lists, b0, b1, b2, b3, f1, f2, s2, s1,
    o0, o1, o2, o3, scratch, f0,
):
    outs = (o0, o1, o2, o3)
    width = f1.shape[1]
    quarter = width // len(outs)
    f0[...] = whole(got, 0)
    placed = place(0, counts, lists, width)
    red = lessened(0, f0[...], recv, parents, placed, (b0, b1, b2, b3), 0, scratch)
    for k, out in enumerate(outs):
        target = lax.rem(lax.axis_index("panel") + k, len(outs))
        cols = pl.ds(pl.multiple_of(target * quarter, quarter), quarter)
        out[:, :width] = red
        for index, value in enumerate(
            (f0[:, cols], f1[:, cols], f2[:, cols], s2[0, :, cols], s1[0, :, cols])
        ):
            out[:, width + index * quarter : width + (index + 1) * quarter] = value


def last_body(*refs):
    panels = (len(refs) - 3) // 2
    ends, cols = refs[:panels], refs[panels : 2 * panels]
    fwd, sol, reds = refs[2 * panels :]
    width = reds.shape[1]
    quarter = width // panels
    rows = ends[0].shape[0]
    for k in range(panels):
        q = order(k, panels)
        span = pl.ds(pl.multiple_of(q * rows, rows), rows)
        reds[span] = ends[k][:, :width]
        for index, (out, level) in enumerate(
            ((fwd, 0), (fwd, 1), (fwd, 2), (sol, 2), (sol, 1))
        ):
            out[level, 0, span] = ends[k][:, width + index * quarter : width + (index + 1) * quarter]
    total = None
    for k in range(panels):
        q = order(k, panels)
        part = mul(
            reds[:, pl.ds(pl.multiple_of(q * quarter, quarter), quarter)], cols[k][:, -quarter:]
        )
        total = part if total is None else total + part
    sol[0, 0] = total.astype(BF)


def local(rhs, inv_diag, coupling, row_lists, parents, counts):
    panels = lax.axis_size("panel")
    rows = rhs.shape[2] // panels
    mid = (GROUP, rows, inv_diag.shape[3])
    after = lax.optimization_barrier

    def shifted(x, k):
        return lax.ppermute(x, "panel", [(i, (i + k) % panels) for i in range(panels)])

    def placement(level, counts):
        return call(
            functools.partial(place_body, level),
            sds(inv_diag.shape[3], row_lists.shape[2]),
            counts, row_lists,
            specs=[SMEM, VMEM],
        )

    half = coupling.shape[3]
    tall = rhs.shape[3]
    half = coupling.shape[3]
    tall = rhs.shape[3]
    width = inv_diag.shape[3]

    def exchange(x, axes, weights=(), shifts=()):
        x, *weights = after((x, *weights))
        moved = [shifted(w, k) for w, k in zip(weights, shifts)]
        x = lax.all_to_all(x, axes, 0, 0)
        return after((x, *moved))

    own, c1, *packs = call(
        pack_body,
        [sds(tall, half), sds(tall, panels * half)]
        + [sds(2 * rhs.shape[2] + tall, half)] * (panels - 1),
        rhs, coupling, specs=[HBM] * 2,
        scratch=[pltpu.SemaphoreType.DMA((4 * panels - 2,))],
    )
    packs = [shifted(x, k) for k, x in enumerate(packs, 1)]
    base, in1, in2 = (inv_diag[level, 0] for level in range(3))
    packs[0], c1 = after((packs[0], c1))
    c11, c12, c13 = (shifted(c1, k) for k in range(1, panels))
    placed0 = placement(0, counts)
    base, placed0, in1, in2 = after((base, placed0, in1, in2))
    send = call(
        first_body, sds(panels, 14, rows, half), rhs, own, *packs, base,
    )
    got = lax.all_to_all(send, "panel", 0, 0)
    got, c11, c12, c13 = after((got, c11, c12, c13))
    touched = pltpu.VMEM((rows, panels * half), BF)
    wide = pltpu.VMEM((rows, panels * half), F32)
    e = call(up0_body, sds(*mid), counts, got, placed0, specs=[SMEM] + [VMEM] * 2)

    def fold(e, level, table):
        return call(
            functools.partial(fold_body, level), sds(*mid), table, e,
            specs=[SMEM, VMEM], scratch=[pltpu.VMEM((GROUP + 1, *mid[1:]), F32)],
        )

    def route(s, level, table):
        return call(functools.partial(route_body, level), sds(*mid), table, s, specs=[SMEM, VMEM])

    e, in11, in13 = exchange(e, "z", [in1, in1], [1, 3])
    e = fold(e, 0, parents)
    e, in12 = exchange(e, ("x", "core"), [in1], [2])
    level1 = (in1, in11, in12, in13, c1, c11, c12, c13)
    f1, e, keep = call(
        up1_body, [sds(*mid[1:]), sds(*mid), sds(panels, tall, width + panels * half)],
        counts, e, got, row_lists, *level1,
        specs=[SMEM] + [VMEM] * 11, outs_at=[VMEM, VMEM, HBM],
        scratch=[wide, pltpu.SemaphoreType.DMA((panels, 2))],
    )
    e, in21, in23 = exchange(e, "z", [in2, in2], [1, 3])
    e = fold(e, 1, parents)
    e, in22 = exchange(e, ("x", "core"), [in2], [2])
    f2, s2 = call(
        top_body, (sds(*mid[1:]), sds(*mid)), e, got, in2, in21, in22, in23
    )
    s, inv_late, near_coupling = after((s2, inv_diag, coupling))
    w0 = call(
        last_weights_body, [sds(tall, panels * half + tall)] * panels, near_coupling, inv_late,
        specs=[HBM] * 2, outs_at=HBM,
        scratch=[pltpu.SemaphoreType.DMA((panels * (panels + 1),))],
    )
    s = lax.all_to_all(s, "z", 0, 0)
    s, *w0 = after((s, *w0))
    s = route(s, 1, parents)
    s, w01, w03 = exchange(s, ("x", "core"), [w0[1], w0[3]], [1, 3])
    s1 = call(
        down1_body, sds(*mid), parents, counts, s, f1, row_lists, keep,
        specs=[SMEM] * 2 + [VMEM] * 3 + [HBM],
        scratch=[
            touched, pltpu.VMEM(mid[1:], BF), pltpu.VMEM(keep.shape, BF),
            pltpu.SemaphoreType.DMA((panels, 2)),
        ],
    )
    s, far2 = after((s1, w0[2]))
    w02 = shifted(far2, 2)
    s = lax.all_to_all(s, "z", 0, 0)
    w0 = (w0[0], w01, w02, w03)
    s = route(s, 0, parents)
    s = lax.all_to_all(s, ("x", "core"), 0, 0)
    ends = call(
        down0_body, [sds(rows, mid[2] + 5 * tall)] * panels,
        parents, counts, s, got, row_lists, *w0, f1, f2, s2, s1,
        specs=[SMEM] * 2 + [VMEM] * 11, scratch=[touched, pltpu.VMEM(mid[1:], BF)],
    )
    ends = [ends[0]] + [shifted(x, k) for k, x in enumerate(ends[1:], 1)]
    return call(
        last_body, (sds(*rhs.shape), sds(*rhs.shape)), *ends, *w0,
        scratch=[pltpu.VMEM((rhs.shape[2], mid[2]), BF)],
    )


def solution(mesh):
    leaves, panels = mesh.shape["leaf"], mesh.shape["panel"]
    inner = Mesh(
        mesh.devices.reshape(leaves // GROUP, GROUP // 2, 2, panels), ("z", "x", "core", "panel")
    )
    leaf = ("z", "x", "core")
    placed = (
        P(None, leaf, None, "panel"),
        P(None, leaf, "panel", None),
        P(None, leaf, None, "panel"),
        P(),
        P(),
        P(),
    )
    return jax.shard_map(
        local,
        mesh=inner,
        in_specs=placed,
        out_specs=(P(None, leaf, None, "panel"), P(None, leaf, None, "panel")),
        check_vma=False,
    )
```

```python
import functools

import jax
import jax.numpy as jnp
from jax import lax
from jax.experimental import pallas as pl
from jax.experimental.pallas import tpu as pltpu
from jax.sharding import Mesh, PartitionSpec as P

BF = jnp.bfloat16
F32 = jnp.float32
GROUP = 8
VMEM = pl.BlockSpec(memory_space=pltpu.VMEM)
SMEM = pl.BlockSpec(memory_space=pltpu.SMEM)
HBM = pl.BlockSpec(memory_space=pltpu.HBM)
PARAMS = pltpu.CompilerParams(vmem_limit_bytes=8 * 1024 * 1024)
NT = (((1,), (1,)), ((), ()))
NN = (((1,), (0,)), ((), ()))


def mul_t(a, b):
    return lax.dot_general(a, b, NT, preferred_element_type=F32)


def mul(a, b):
    return lax.dot_general(a, b, NN, preferred_element_type=F32)


def call(body, outs, *args, specs=None, outs_at=VMEM, scratch=()):
    specs = [VMEM] * len(args) if specs is None else specs
    args = [far(x) if spec is HBM else x for x, spec in zip(args, specs)]
    return pl.pallas_call(
        body,
        out_shape=tuple(outs) if isinstance(outs, list) else outs,
        in_specs=specs,
        out_specs=outs_at if isinstance(outs_at, list) else jax.tree.map(lambda _: outs_at, outs),
        scratch_shapes=list(scratch),
        compiler_params=PARAMS,
    )(*args)


def far(x):
    return pltpu.with_memory_space_constraint(x, pltpu.HBM)


def sds(*shape, dtype=BF):
    return jax.ShapeDtypeStruct(shape, dtype)


def leaf_place():
    z = lax.axis_index("z")
    lane = lax.axis_index("x") * lax.axis_size("core") + lax.axis_index("core")
    return z, lane, z * GROUP + lane


def order(k, panels):
    return lax.rem(lax.axis_index("panel") + panels - k, panels)


def pack_body(rhs, coupling, own, beside, *refs):
    *outs, sems = refs
    panels = len(outs) + 1
    rows, quarter = rhs.shape[2:]
    width = coupling.shape[-1]
    pairs = []
    for k, out in enumerate((own, *outs)):
        target = lax.rem(lax.axis_index("panel") + k, panels)
        start = pl.multiple_of(target * quarter, quarter)
        source = coupling.at[0, 0, pl.ds(start, quarter)]
        if k == 0:
            pairs.append((source, out))
            continue
        pairs.append((source, out.at[pl.ds(2 * rows, quarter)]))
        for half in range(2):
            lanes = pl.ds(half * width, width)
            pairs.append((rhs.at[0, 0, :, lanes], out.at[pl.ds(half * rows, rows)]))
    for part in range(panels):
        source = coupling.at[1, 0, pl.ds(part * quarter, quarter)]
        pairs.append((source, beside.at[:, pl.ds(part * width, width)]))
    copies = [pltpu.make_async_copy(a, b, sems.at[i]) for i, (a, b) in enumerate(pairs)]
    for copy in copies:
        copy.start()
    for copy in copies:
        copy.wait()


def last_weights_body(coupling, inv, *refs):
    *outs, sems = refs
    rows = inv.shape[2]
    width = coupling.shape[-1]
    parts = len(outs)
    copies = []
    for k, out in enumerate(outs):
        target = lax.rem(lax.axis_index("panel") + k, parts)
        for part in range(parts):
            source = coupling.at[0, 0, pl.ds(part * rows, rows)]
            copies.append((source, out.at[:, pl.ds(part * width, width)]))
        cols = pl.ds(pl.multiple_of(target * rows, rows), rows)
        copies.append((inv.at[0, 0, :, cols], out.at[:, pl.ds(parts * width, rows)]))
    copies = [pltpu.make_async_copy(a, b, sems.at[i]) for i, (a, b) in enumerate(copies)]
    for copy in copies:
        copy.start()
    for copy in copies:
        copy.wait()


def first_body(rhs, own, m1, m2, m3, inv, send):
    panels = send.shape[0]
    rows, quarter = rhs.shape[2:]
    total = None
    for k, ref in enumerate((rhs, m1, m2, m3)):
        q = order(k, panels)
        block = rhs[0, 0] if k == 0 else jnp.concatenate([ref[:rows], ref[rows : 2 * rows]], axis=1)
        part = mul_t(block, inv[:, pl.ds(pl.multiple_of(q * quarter, quarter), quarter)])
        total = part if total is None else total + part
    f = total.astype(BF)
    few = rows // panels
    for k, ref in enumerate((own, m1, m2, m3)):
        q = order(k, panels)
        part = mul(f, own[...] if k == 0 else ref[2 * rows :])
        high = part.astype(BF)
        low = (part - high.astype(F32)).astype(BF)
        for d in range(panels):
            send[d, q] = high[d * few : (d + 1) * few]
            send[d, panels + q] = low[d * few : (d + 1) * few]
    for d in range(panels):
        span = slice(d * few, (d + 1) * few)
        for index, value in enumerate((f[span], rhs[1, 0, span], rhs[2, 0, span])):
            send[d, 2 * panels + 2 * index] = value[:, :128]
            send[d, 2 * panels + 2 * index + 1] = value[:, 128:]


def place(level, counts, lists, rows):
    _, _, leaf = leaf_place()
    mine = lists[level, pl.ds(leaf, 1), :]
    shape = (rows, lists.shape[-1])
    row = lax.broadcasted_iota(jnp.int32, shape, 0)
    col = lax.broadcasted_iota(jnp.int32, shape, 1)
    return jnp.where((row == mine) & (col < counts[level, leaf]), 1.0, 0.0).astype(BF)


def laid_out(level, u, placed, counts):
    _, _, leaf = leaf_place()
    col = lax.broadcasted_iota(jnp.int32, u.shape, 1)
    u = jnp.where(col < counts[level, leaf], u, 0.0).astype(BF)
    return mul_t(u, placed).astype(BF)


def whole(got, index):
    panels = got.shape[0]
    first = 2 * panels + 2 * index
    return jnp.concatenate(
        [got[q, first + half] for q in range(panels) for half in range(2)], axis=1
    )


def up0_body(counts, got, lists, out):
    placed = place(0, counts, lists, out.shape[2])
    panels = got.shape[0]
    pieces = []
    for q in range(panels):
        total = None
        for source in range(panels):
            part = got[source, q].astype(F32) + got[source, panels + q].astype(F32)
            total = part if total is None else total + part
        pieces.append(total)
    e = laid_out(0, jnp.concatenate(pieces, axis=1), placed, counts)
    for d in range(out.shape[0]):
        out[d] = e


def summed(recv):
    total = recv[0].astype(F32)
    for j in range(1, recv.shape[0]):
        total = total + recv[j].astype(F32)
    return total


def forward(resid, blocks, out):
    rows, cols = blocks[0].shape[0], out.shape[1]
    for k, ref in enumerate(blocks):
        start = pl.multiple_of(order(k, len(blocks)) * rows, rows)
        out[:, pl.ds(start, rows)] = mul_t(resid, ref[:, :cols]).astype(BF)
    return out[...]


def backward(reduced, blocks):
    rows, cols = blocks[0].shape[0], reduced.shape[1]
    total = None
    for k, ref in enumerate(blocks):
        start = pl.multiple_of(order(k, len(blocks)) * rows, rows)
        part = mul(reduced[:, pl.ds(start, rows)], ref[:, :cols])
        total = part if total is None else total + part
    return total.astype(BF)


def coupled(f, blocks, first, out):
    rows = blocks[0].shape[0]
    parts = f.shape[1] // rows
    width = out.shape[1] // len(blocks)
    for k, ref in enumerate(blocks):
        total = None
        for part in range(parts):
            lanes = slice(first + part * width, first + (part + 1) * width)
            term = mul(f[:, part * rows : (part + 1) * rows], ref[:, lanes])
            total = term if total is None else total + term
        out[:, pl.ds(pl.multiple_of(order(k, len(blocks)) * width, width), width)] = total


def lessened(level, f, recv, parents, placed, blocks, first, picked):
    _, _, leaf = leaf_place()
    above = recv[lax.rem(parents[level, leaf], GROUP)]
    picked[...] = mul(above, placed).astype(BF)
    rows = blocks[0].shape[0]
    width = picked.shape[1] // len(blocks)
    pieces = []
    for part in range(f.shape[1] // rows):
        lanes = slice(first + part * width, first + (part + 1) * width)
        total = None
        for k, ref in enumerate(blocks):
            start = pl.multiple_of(order(k, len(blocks)) * width, width)
            term = mul_t(picked[:, pl.ds(start, width)], ref[:, lanes])
            total = term if total is None else total + term
        pieces.append(total)
    return (f.astype(F32) - jnp.concatenate(pieces, axis=1)).astype(BF)


def to_all(out, value):
    for d in range(out.shape[0]):
        out[d] = value


def up1_body(counts, recv, got, lists, i0, i1, i2, i3, c0, c1, c2, c3, fout, out, keep, scratch, sems):
    inverse, blocks = (i0, i1, i2, i3), (c0, c1, c2, c3)
    cols = i0.shape[1]
    copies = []
    for k in range(len(blocks)):
        for part, (source, span) in enumerate(
            ((inverse[k], pl.ds(0, cols)), (blocks[k], pl.ds(cols, c0.shape[1])))
        ):
            copies.append(pltpu.make_async_copy(source, keep.at[k, :, span], sems.at[k, part]))
    for copy in copies:
        copy.start()
    resid = (whole(got, 1).astype(F32) - summed(recv)).astype(BF)
    placed = place(1, counts, lists, fout.shape[1])
    f = forward(resid, inverse, fout)
    coupled(f, blocks, 0, scratch)
    to_all(out, laid_out(1, scratch[...], placed, counts))
    for copy in copies:
        copy.wait()


def top_body(recv, got, i0, i1, i2, i3, fout, out):
    resid = (whole(got, 2).astype(F32) - summed(recv)).astype(BF)
    blocks = (i0, i1, i2, i3)
    forward(resid, blocks, fout)
    to_all(out, backward(fout, blocks))


def fold_body(level, parents, blocks, out, acc):
    z, lane, _ = leaf_place()
    acc[...] = jnp.zeros_like(acc)
    for j in range(blocks.shape[0]):
        parent = parents[level, j * GROUP + lane]
        d = jnp.where(lax.div(parent, GROUP) == z, lax.rem(parent, GROUP), GROUP)
        acc[d] = acc[d] + blocks[j].astype(F32)
    for d in range(out.shape[0]):
        out[d] = acc[d].astype(BF)


def route_body(level, parents, blocks, out):
    z, _, _ = leaf_place()
    for d in range(out.shape[0]):
        out[d] = blocks[lax.div(parents[level, z * GROUP + d], GROUP)]


def down1_body(parents, counts, recv, f, lists, keep, out, picked, red, held, sems):
    cols = red.shape[1]
    parts = (pl.ds(cols, held.shape[2] - cols), pl.ds(0, cols))
    copies = [
        [
            pltpu.make_async_copy(keep.at[k, :, span], held.at[k, :, span], sems.at[k, part])
            for k in range(keep.shape[0])
        ]
        for part, span in enumerate(parts)
    ]
    for copy in copies[0] + copies[1]:
        copy.start()
    blocks = [held.at[k] for k in range(keep.shape[0])]
    placed = place(1, counts, lists, cols)
    for copy in copies[0]:
        copy.wait()
    red[...] = lessened(1, f[...], recv, parents, placed, blocks, cols, picked)
    for copy in copies[1]:
        copy.wait()
    to_all(out, backward(red, blocks))


def down0_body(
    parents, counts, recv, got, lists, b0, b1, b2, b3, f1, f2, s2, s1,
    o0, o1, o2, o3, scratch, f0,
):
    outs = (o0, o1, o2, o3)
    width = f1.shape[1]
    quarter = width // len(outs)
    f0[...] = whole(got, 0)
    placed = place(0, counts, lists, width)
    red = lessened(0, f0[...], recv, parents, placed, (b0, b1, b2, b3), 0, scratch)
    for k, out in enumerate(outs):
        target = lax.rem(lax.axis_index("panel") + k, len(outs))
        cols = pl.ds(pl.multiple_of(target * quarter, quarter), quarter)
        out[:, :width] = red
        for index, value in enumerate(
            (f0[:, cols], f1[:, cols], f2[:, cols], s2[0, :, cols], s1[0, :, cols])
        ):
            out[:, width + index * quarter : width + (index + 1) * quarter] = value


def last_body(*refs):
    panels = (len(refs) - 3) // 2
    ends, cols = refs[:panels], refs[panels : 2 * panels]
    fwd, sol, reds = refs[2 * panels :]
    width = reds.shape[1]
    quarter = width // panels
    rows = ends[0].shape[0]
    for k in range(panels):
        q = order(k, panels)
        span = pl.ds(pl.multiple_of(q * rows, rows), rows)
        reds[span] = ends[k][:, :width]
        for index, (out, level) in enumerate(
            ((fwd, 0), (fwd, 1), (fwd, 2), (sol, 2), (sol, 1))
        ):
            out[level, 0, span] = ends[k][:, width + index * quarter : width + (index + 1) * quarter]
    total = None
    for k in range(panels):
        q = order(k, panels)
        part = mul(
            reds[:, pl.ds(pl.multiple_of(q * quarter, quarter), quarter)], cols[k][:, -quarter:]
        )
        total = part if total is None else total + part
    sol[0, 0] = total.astype(BF)


def local(rhs, inv_diag, coupling, row_lists, parents, counts):
    panels = lax.axis_size("panel")
    rows = rhs.shape[2] // panels
    mid = (GROUP, rows, inv_diag.shape[3])
    after = lax.optimization_barrier

    def shifted(x, k):
        return lax.ppermute(x, "panel", [(i, (i + k) % panels) for i in range(panels)])

    half = coupling.shape[3]
    tall = rhs.shape[3]
    half = coupling.shape[3]
    tall = rhs.shape[3]
    width = inv_diag.shape[3]

    def exchange(x, axes, weights=(), shifts=()):
        x, *weights = after((x, *weights))
        moved = [shifted(w, k) for w, k in zip(weights, shifts)]
        x = lax.all_to_all(x, axes, 0, 0)
        return after((x, *moved))

    own, c1, *packs = call(
        pack_body,
        [sds(tall, half), sds(tall, panels * half)]
        + [sds(2 * rhs.shape[2] + tall, half)] * (panels - 1),
        rhs, coupling, specs=[HBM] * 2,
        scratch=[pltpu.SemaphoreType.DMA((4 * panels - 2,))],
    )
    packs = [shifted(x, k) for k, x in enumerate(packs, 1)]
    base, in1, in2 = (inv_diag[level, 0] for level in range(3))
    packs[0], c1 = after((packs[0], c1))
    c11, c12, c13 = (shifted(c1, k) for k in range(1, panels))
    base, in1, in2 = after((base, in1, in2))
    send = call(
        first_body, sds(panels, 14, rows, half), rhs, own, *packs, base,
    )
    got = lax.all_to_all(send, "panel", 0, 0)
    got, c11, c12, c13 = after((got, c11, c12, c13))
    touched = pltpu.VMEM((rows, panels * half), BF)
    wide = pltpu.VMEM((rows, panels * half), F32)
    e = call(up0_body, sds(*mid), counts, got, row_lists, specs=[SMEM] + [VMEM] * 2)

    def fold(e, level, table):
        return call(
            functools.partial(fold_body, level), sds(*mid), table, e,
            specs=[SMEM, VMEM], scratch=[pltpu.VMEM((GROUP + 1, *mid[1:]), F32)],
        )

    def route(s, level, table):
        return call(functools.partial(route_body, level), sds(*mid), table, s, specs=[SMEM, VMEM])

    e, in11, in13 = exchange(e, "z", [in1, in1], [1, 3])
    e = fold(e, 0, parents)
    e, in12 = exchange(e, ("x", "core"), [in1], [2])
    level1 = (in1, in11, in12, in13, c1, c11, c12, c13)
    f1, e, keep = call(
        up1_body, [sds(*mid[1:]), sds(*mid), sds(panels, tall, width + panels * half)],
        counts, e, got, row_lists, *level1,
        specs=[SMEM] + [VMEM] * 11, outs_at=[VMEM, VMEM, HBM],
        scratch=[wide, pltpu.SemaphoreType.DMA((panels, 2))],
    )
    e, in21, in23 = exchange(e, "z", [in2, in2], [1, 3])
    e = fold(e, 1, parents)
    e, in22 = exchange(e, ("x", "core"), [in2], [2])
    f2, s2 = call(
        top_body, (sds(*mid[1:]), sds(*mid)), e, got, in2, in21, in22, in23
    )
    s, inv_late, near_coupling = after((s2, inv_diag, coupling))
    w0 = call(
        last_weights_body, [sds(tall, panels * half + tall)] * panels, near_coupling, inv_late,
        specs=[HBM] * 2, outs_at=HBM,
        scratch=[pltpu.SemaphoreType.DMA((panels * (panels + 1),))],
    )
    w0 = [*w0]
    s = lax.all_to_all(s, "z", 0, 0)
    w01, w03 = shifted(w0[1], 1), shifted(w0[3], 3)
    s, w0[0], w0[2] = after((s, w0[0], w0[2]))
    s = route(s, 1, parents)
    s = lax.all_to_all(s, ("x", "core"), 0, 0)
    s, w01, w03 = after((s, w01, w03))
    s1 = call(
        down1_body, sds(*mid), parents, counts, s, f1, row_lists, keep,
        specs=[SMEM] * 2 + [VMEM] * 3 + [HBM],
        scratch=[
            touched, pltpu.VMEM(mid[1:], BF), pltpu.VMEM(keep.shape, BF),
            pltpu.SemaphoreType.DMA((panels, 2)),
        ],
    )
    s, far2 = after((s1, w0[2]))
    w02 = shifted(far2, 2)
    s = lax.all_to_all(s, "z", 0, 0)
    w0 = (w0[0], w01, w02, w03)
    s = route(s, 0, parents)
    s = lax.all_to_all(s, ("x", "core"), 0, 0)
    ends = call(
        down0_body, [sds(rows, mid[2] + 5 * tall)] * panels,
        parents, counts, s, got, row_lists, *w0, f1, f2, s2, s1,
        specs=[SMEM] * 2 + [VMEM] * 11, scratch=[touched, pltpu.VMEM(mid[1:], BF)],
    )
    ends = [ends[0]] + [shifted(x, k) for k, x in enumerate(ends[1:], 1)]
    return call(
        last_body, (sds(*rhs.shape), sds(*rhs.shape)), *ends, *w0,
        scratch=[pltpu.VMEM((rhs.shape[2], mid[2]), BF)],
    )


def solution(mesh):
    leaves, panels = mesh.shape["leaf"], mesh.shape["panel"]
    inner = Mesh(
        mesh.devices.reshape(leaves // GROUP, GROUP // 2, 2, panels), ("z", "x", "core", "panel")
    )
    leaf = ("z", "x", "core")
    placed = (
        P(None, leaf, None, "panel"),
        P(None, leaf, "panel", None),
        P(None, leaf, None, "panel"),
        P(),
        P(),
        P(),
    )
    return jax.shard_map(
        local,
        mesh=inner,
        in_specs=placed,
        out_specs=(P(None, leaf, None, "panel"), P(None, leaf, None, "panel")),
        check_vma=False,
    )
```

```python
import functools

import jax
import jax.numpy as jnp
from jax import lax
from jax.experimental import pallas as pl
from jax.experimental.pallas import tpu as pltpu
from jax.sharding import Mesh, PartitionSpec as P

BF = jnp.bfloat16
F32 = jnp.float32
GROUP = 8
VMEM = pl.BlockSpec(memory_space=pltpu.VMEM)
SMEM = pl.BlockSpec(memory_space=pltpu.SMEM)
HBM = pl.BlockSpec(memory_space=pltpu.HBM)
PARAMS = pltpu.CompilerParams(vmem_limit_bytes=8 * 1024 * 1024)
NT = (((1,), (1,)), ((), ()))
NN = (((1,), (0,)), ((), ()))


def mul_t(a, b):
    return lax.dot_general(a, b, NT, preferred_element_type=F32)


def mul(a, b):
    return lax.dot_general(a, b, NN, preferred_element_type=F32)


def call(body, outs, *args, specs=None, outs_at=VMEM, scratch=()):
    specs = [VMEM] * len(args) if specs is None else specs
    args = [far(x) if spec is HBM else x for x, spec in zip(args, specs)]
    return pl.pallas_call(
        body,
        out_shape=tuple(outs) if isinstance(outs, list) else outs,
        in_specs=specs,
        out_specs=outs_at if isinstance(outs_at, list) else jax.tree.map(lambda _: outs_at, outs),
        scratch_shapes=list(scratch),
        compiler_params=PARAMS,
    )(*args)


def far(x):
    return pltpu.with_memory_space_constraint(x, pltpu.HBM)


def sds(*shape, dtype=BF):
    return jax.ShapeDtypeStruct(shape, dtype)


def leaf_place():
    z = lax.axis_index("z")
    lane = lax.axis_index("x") * lax.axis_size("core") + lax.axis_index("core")
    return z, lane, z * GROUP + lane


def order(k, panels):
    return lax.rem(lax.axis_index("panel") + panels - k, panels)


def pack_body(rhs, coupling, own, beside, *refs):
    *outs, sems = refs
    panels = len(outs) + 1
    rows, quarter = rhs.shape[2:]
    width = coupling.shape[-1]
    pairs = []
    for k, out in enumerate((own, *outs)):
        target = lax.rem(lax.axis_index("panel") + k, panels)
        start = pl.multiple_of(target * quarter, quarter)
        source = coupling.at[0, 0, pl.ds(start, quarter)]
        if k == 0:
            pairs.append((source, out))
            continue
        pairs.append((source, out.at[pl.ds(2 * rows, quarter)]))
        for half in range(2):
            lanes = pl.ds(half * width, width)
            pairs.append((rhs.at[0, 0, :, lanes], out.at[pl.ds(half * rows, rows)]))
    for part in range(panels):
        source = coupling.at[1, 0, pl.ds(part * quarter, quarter)]
        pairs.append((source, beside.at[:, pl.ds(part * width, width)]))
    copies = [pltpu.make_async_copy(a, b, sems.at[i]) for i, (a, b) in enumerate(pairs)]
    for copy in copies:
        copy.start()
    for copy in copies:
        copy.wait()


def last_weights_body(coupling, inv, *refs):
    *outs, sems = refs
    rows = inv.shape[2]
    width = coupling.shape[-1]
    parts = len(outs)
    copies = []
    for k, out in enumerate(outs):
        target = lax.rem(lax.axis_index("panel") + k, parts)
        for part in range(parts):
            source = coupling.at[0, 0, pl.ds(part * rows, rows)]
            copies.append((source, out.at[:, pl.ds(part * width, width)]))
        cols = pl.ds(pl.multiple_of(target * rows, rows), rows)
        for start in range(parts * width, out.shape[1], rows):
            copies.append((inv.at[0, 0, :, cols], out.at[:, pl.ds(start, rows)]))
    copies = [pltpu.make_async_copy(a, b, sems.at[i]) for i, (a, b) in enumerate(copies)]
    for copy in copies:
        copy.start()
    for copy in copies:
        copy.wait()


def first_body(rhs, own, m1, m2, m3, inv, send):
    panels = send.shape[0]
    rows, quarter = rhs.shape[2:]
    total = None
    for k, ref in enumerate((rhs, m1, m2, m3)):
        q = order(k, panels)
        block = rhs[0, 0] if k == 0 else jnp.concatenate([ref[:rows], ref[rows : 2 * rows]], axis=1)
        part = mul_t(block, inv[:, pl.ds(pl.multiple_of(q * quarter, quarter), quarter)])
        total = part if total is None else total + part
    f = total.astype(BF)
    few = rows // panels
    for k, ref in enumerate((own, m1, m2, m3)):
        q = order(k, panels)
        part = mul(f, own[...] if k == 0 else ref[2 * rows :])
        high = part.astype(BF)
        low = (part - high.astype(F32)).astype(BF)
        for d in range(panels):
            send[d, q] = high[d * few : (d + 1) * few]
            send[d, panels + q] = low[d * few : (d + 1) * few]
    for d in range(panels):
        span = slice(d * few, (d + 1) * few)
        for index, value in enumerate((f[span], rhs[1, 0, span], rhs[2, 0, span])):
            send[d, 2 * panels + 2 * index] = value[:, :128]
            send[d, 2 * panels + 2 * index + 1] = value[:, 128:]


def place(level, counts, lists, rows):
    _, _, leaf = leaf_place()
    mine = lists[level, pl.ds(leaf, 1), :]
    shape = (rows, lists.shape[-1])
    row = lax.broadcasted_iota(jnp.int32, shape, 0)
    col = lax.broadcasted_iota(jnp.int32, shape, 1)
    return jnp.where((row == mine) & (col < counts[level, leaf]), 1.0, 0.0).astype(BF)


def laid_out(level, u, placed, counts):
    _, _, leaf = leaf_place()
    col = lax.broadcasted_iota(jnp.int32, u.shape, 1)
    u = jnp.where(col < counts[level, leaf], u, 0.0).astype(BF)
    return mul_t(u, placed).astype(BF)


def whole(got, index):
    panels = got.shape[0]
    first = 2 * panels + 2 * index
    return jnp.concatenate(
        [got[q, first + half] for q in range(panels) for half in range(2)], axis=1
    )


def up0_body(counts, got, lists, out):
    placed = place(0, counts, lists, out.shape[2])
    panels = got.shape[0]
    pieces = []
    for q in range(panels):
        total = None
        for source in range(panels):
            part = got[source, q].astype(F32) + got[source, panels + q].astype(F32)
            total = part if total is None else total + part
        pieces.append(total)
    e = laid_out(0, jnp.concatenate(pieces, axis=1), placed, counts)
    for d in range(out.shape[0]):
        out[d] = e


def summed(recv):
    total = recv[0].astype(F32)
    for j in range(1, recv.shape[0]):
        total = total + recv[j].astype(F32)
    return total


def forward(resid, blocks, out):
    rows, cols = blocks[0].shape[0], out.shape[1]
    for k, ref in enumerate(blocks):
        start = pl.multiple_of(order(k, len(blocks)) * rows, rows)
        out[:, pl.ds(start, rows)] = mul_t(resid, ref[:, :cols]).astype(BF)
    return out[...]


def backward(reduced, blocks):
    rows, cols = blocks[0].shape[0], reduced.shape[1]
    total = None
    for k, ref in enumerate(blocks):
        start = pl.multiple_of(order(k, len(blocks)) * rows, rows)
        part = mul(reduced[:, pl.ds(start, rows)], ref[:, :cols])
        total = part if total is None else total + part
    return total.astype(BF)


def coupled(f, blocks, first, out):
    rows = blocks[0].shape[0]
    parts = f.shape[1] // rows
    width = out.shape[1] // len(blocks)
    for k, ref in enumerate(blocks):
        total = None
        for part in range(parts):
            lanes = slice(first + part * width, first + (part + 1) * width)
            term = mul(f[:, part * rows : (part + 1) * rows], ref[:, lanes])
            total = term if total is None else total + term
        out[:, pl.ds(pl.multiple_of(order(k, len(blocks)) * width, width), width)] = total


def lessened(level, f, recv, parents, placed, blocks, first, picked, place_of):
    _, _, leaf = leaf_place()
    above = recv[lax.rem(parents[level, leaf], GROUP)]
    picked[...] = mul(above, placed).astype(BF)
    rows = blocks[0].shape[0]
    width = picked.shape[1] // len(blocks)
    pieces = []
    for part in range(f.shape[1] // rows):
        lanes = slice(first + part * width, first + (part + 1) * width)
        total = None
        for k, ref in enumerate(blocks):
            start = pl.multiple_of(place_of(k) * width, width)
            term = mul_t(picked[:, pl.ds(start, width)], ref[:, lanes])
            total = term if total is None else total + term
        pieces.append(total)
    return (f.astype(F32) - jnp.concatenate(pieces, axis=1)).astype(BF)


def to_all(out, value):
    for d in range(out.shape[0]):
        out[d] = value


def up1_body(counts, recv, got, lists, i0, i1, i2, i3, c0, c1, c2, c3, fout, out, keep, scratch, sems):
    inverse, blocks = (i0, i1, i2, i3), (c0, c1, c2, c3)
    cols = i0.shape[1]
    copies = []
    for k in range(len(blocks)):
        for part, (source, span) in enumerate(
            ((inverse[k], pl.ds(0, cols)), (blocks[k], pl.ds(cols, c0.shape[1])))
        ):
            target = keep.at[order(k, len(blocks)), :, span]
            copies.append(pltpu.make_async_copy(source, target, sems.at[k, part]))
    for copy in copies:
        copy.start()
    resid = (whole(got, 1).astype(F32) - summed(recv)).astype(BF)
    placed = place(1, counts, lists, fout.shape[1])
    f = forward(resid, inverse, fout)
    coupled(f, blocks, 0, scratch)
    to_all(out, laid_out(1, scratch[...], placed, counts))
    for copy in copies:
        copy.wait()


def top_body(recv, got, i0, i1, i2, i3, fout, out):
    resid = (whole(got, 2).astype(F32) - summed(recv)).astype(BF)
    blocks = (i0, i1, i2, i3)
    forward(resid, blocks, fout)
    to_all(out, backward(fout, blocks))


def fold_body(level, parents, blocks, out, acc):
    z, lane, _ = leaf_place()
    acc[...] = jnp.zeros_like(acc)
    for j in range(blocks.shape[0]):
        parent = parents[level, j * GROUP + lane]
        d = jnp.where(lax.div(parent, GROUP) == z, lax.rem(parent, GROUP), GROUP)
        acc[d] = acc[d] + blocks[j].astype(F32)
    for d in range(out.shape[0]):
        out[d] = acc[d].astype(BF)


def route_body(level, parents, blocks, out):
    z, _, _ = leaf_place()
    for d in range(out.shape[0]):
        out[d] = blocks[lax.div(parents[level, z * GROUP + d], GROUP)]


def down1_body(parents, counts, recv, f, lists, keep, out, picked, red, held, sems):
    cols = red.shape[1]
    rows = keep.shape[1]
    panels = keep.shape[0]

    def copy(q, part, span):
        return pltpu.make_async_copy(keep.at[q, :, span], held.at[q, :, span], sems.at[q, part])

    couplings = [copy(q, 0, pl.ds(cols, held.shape[2] - cols)) for q in range(panels)]
    inverse = [copy(q, 1, pl.ds(0, (q + 1) * rows)) for q in range(panels)]
    for started in couplings + inverse:
        started.start()
    blocks = [held.at[q] for q in range(panels)]
    placed = place(1, counts, lists, cols)
    for started in couplings:
        started.wait()
    red[...] = lessened(1, f[...], recv, parents, placed, blocks, cols, picked, lambda q: q)
    for started in inverse:
        started.wait()
    pieces = []
    for part in range(panels):
        lanes = slice(part * rows, (part + 1) * rows)
        total = None
        for q in range(part, panels):
            term = mul(red[:, q * rows : (q + 1) * rows], held[q, :, lanes])
            total = term if total is None else total + term
        pieces.append(total)
    to_all(out, jnp.concatenate(pieces, axis=1).astype(BF))


def down0_body(
    parents, counts, recv, got, lists, b0, b1, b2, b3, f1, f2, s2, s1,
    o0, o1, o2, o3, scratch, f0,
):
    outs = (o0, o1, o2, o3)
    width = f1.shape[1]
    quarter = width // len(outs)
    f0[...] = whole(got, 0)
    placed = place(0, counts, lists, width)
    red = lessened(0, f0[...], recv, parents, placed, (b0, b1, b2, b3), 0, scratch,
        lambda k: order(k, 4),
    )
    for k, out in enumerate(outs):
        target = lax.rem(lax.axis_index("panel") + k, len(outs))
        cols = pl.ds(pl.multiple_of(target * quarter, quarter), quarter)
        out[:, :width] = red
        for index, value in enumerate(
            (f0[:, cols], f1[:, cols], f2[:, cols], s2[0, :, cols], s1[0, :, cols])
        ):
            out[:, width + index * quarter : width + (index + 1) * quarter] = value


def last_body(*refs):
    panels = (len(refs) - 3) // 2
    ends, cols = refs[:panels], refs[panels : 2 * panels]
    first = cols[0].shape[1] - cols[0].shape[0]
    fwd, sol, reds = refs[2 * panels :]
    width = reds.shape[1]
    quarter = width // panels
    rows = ends[0].shape[0]
    for k in range(panels):
        q = order(k, panels)
        span = pl.ds(pl.multiple_of(q * rows, rows), rows)
        reds[span] = ends[k][:, :width]
        for index, (out, level) in enumerate(
            ((fwd, 0), (fwd, 1), (fwd, 2), (sol, 2), (sol, 1))
        ):
            out[level, 0, span] = ends[k][:, width + index * quarter : width + (index + 1) * quarter]
    total = None
    for k in range(panels):
        q = order(k, panels)
        part = mul(
            reds[:, pl.ds(pl.multiple_of(q * quarter, quarter), quarter)], cols[k][:, first : first + quarter]
        )
        total = part if total is None else total + part
    sol[0, 0] = total.astype(BF)


def local(rhs, inv_diag, coupling, row_lists, parents, counts):
    panels = lax.axis_size("panel")
    rows = rhs.shape[2] // panels
    mid = (GROUP, rows, inv_diag.shape[3])
    after = lax.optimization_barrier

    def shifted(x, k):
        return lax.ppermute(x, "panel", [(i, (i + k) % panels) for i in range(panels)])

    half = coupling.shape[3]
    tall = rhs.shape[3]
    half = coupling.shape[3]
    tall = rhs.shape[3]
    width = inv_diag.shape[3]

    def exchange(x, axes, weights=(), shifts=()):
        x, *weights = after((x, *weights))
        moved = [shifted(w, k) for w, k in zip(weights, shifts)]
        x = lax.all_to_all(x, axes, 0, 0)
        return after((x, *moved))

    own, c1, *packs = call(
        pack_body,
        [sds(tall, half), sds(tall, panels * half)]
        + [sds(2 * rhs.shape[2] + tall, half)] * (panels - 1),
        rhs, coupling, specs=[HBM] * 2,
        scratch=[pltpu.SemaphoreType.DMA((4 * panels - 2,))],
    )
    packs = [shifted(x, k) for k, x in enumerate(packs, 1)]
    base, in1, in2 = (inv_diag[level, 0] for level in range(3))
    packs[0], c1 = after((packs[0], c1))
    c11, c12, c13 = (shifted(c1, k) for k in range(1, panels))
    base, in1, in2 = after((base, in1, in2))
    send = call(
        first_body, sds(panels, 14, rows, half), rhs, own, *packs, base,
    )
    got = lax.all_to_all(send, "panel", 0, 0)
    got, c11, c12, c13 = after((got, c11, c12, c13))
    touched = pltpu.VMEM((rows, panels * half), BF)
    wide = pltpu.VMEM((rows, panels * half), F32)
    e = call(up0_body, sds(*mid), counts, got, row_lists, specs=[SMEM] + [VMEM] * 2)

    def fold(e, level, table):
        return call(
            functools.partial(fold_body, level), sds(*mid), table, e,
            specs=[SMEM, VMEM], scratch=[pltpu.VMEM((GROUP + 1, *mid[1:]), F32)],
        )

    def route(s, level, table):
        return call(functools.partial(route_body, level), sds(*mid), table, s, specs=[SMEM, VMEM])

    e, in11, in13 = exchange(e, "z", [in1, in1], [1, 3])
    e = fold(e, 0, parents)
    e, in12 = exchange(e, ("x", "core"), [in1], [2])
    level1 = (in1, in11, in12, in13, c1, c11, c12, c13)
    f1, e, keep = call(
        up1_body, [sds(*mid[1:]), sds(*mid), sds(panels, tall, width + panels * half)],
        counts, e, got, row_lists, *level1,
        specs=[SMEM] + [VMEM] * 11, outs_at=[VMEM, VMEM, HBM],
        scratch=[wide, pltpu.SemaphoreType.DMA((panels, 2))],
    )
    e, in21, in23 = exchange(e, "z", [in2, in2], [1, 3])
    e = fold(e, 1, parents)
    e, in22 = exchange(e, ("x", "core"), [in2], [2])
    f2, s2 = call(
        top_body, (sds(*mid[1:]), sds(*mid)), e, got, in2, in21, in22, in23
    )
    s, inv_late, near_coupling = after((s2, inv_diag, coupling))
    w0 = call(
        last_weights_body,
        [sds(tall, panels * half + (2 if k == 2 else 1) * tall) for k in range(panels)],
        near_coupling, inv_late,
        specs=[HBM] * 2, outs_at=HBM,
        scratch=[pltpu.SemaphoreType.DMA((panels * (panels + 1) + 1,))],
    )
    w0 = [*w0]
    s = lax.all_to_all(s, "z", 0, 0)
    w01, w03 = shifted(w0[1], 1), shifted(w0[3], 3)
    s, w0[0], w0[2] = after((s, w0[0], w0[2]))
    s = route(s, 1, parents)
    s = lax.all_to_all(s, ("x", "core"), 0, 0)
    s, w01, w03 = after((s, w01, w03))
    s1 = call(
        down1_body, sds(*mid), parents, counts, s, f1, row_lists, keep,
        specs=[SMEM] * 2 + [VMEM] * 3 + [HBM],
        scratch=[
            touched, pltpu.VMEM(mid[1:], BF), pltpu.VMEM(keep.shape, BF),
            pltpu.SemaphoreType.DMA((panels, 2)),
        ],
    )
    s, w02 = exchange(s1, "z", [w0[2]], [2])
    w0 = (w0[0], w01, w02, w03)
    s = route(s, 0, parents)
    s = lax.all_to_all(s, ("x", "core"), 0, 0)
    ends = call(
        down0_body, [sds(rows, mid[2] + 5 * tall)] * panels,
        parents, counts, s, got, row_lists, *w0, f1, f2, s2, s1,
        specs=[SMEM] * 2 + [VMEM] * 11, scratch=[touched, pltpu.VMEM(mid[1:], BF)],
    )
    ends = [ends[0]] + [shifted(x, k) for k, x in enumerate(ends[1:], 1)]
    return call(
        last_body, (sds(*rhs.shape), sds(*rhs.shape)), *ends, *w0,
        scratch=[pltpu.VMEM((rhs.shape[2], mid[2]), BF)],
    )


def solution(mesh):
    leaves, panels = mesh.shape["leaf"], mesh.shape["panel"]
    inner = Mesh(
        mesh.devices.reshape(leaves // GROUP, GROUP // 2, 2, panels), ("z", "x", "core", "panel")
    )
    leaf = ("z", "x", "core")
    placed = (
        P(None, leaf, None, "panel"),
        P(None, leaf, "panel", None),
        P(None, leaf, None, "panel"),
        P(),
        P(),
        P(),
    )
    return jax.shard_map(
        local,
        mesh=inner,
        in_specs=placed,
        out_specs=(P(None, leaf, None, "panel"), P(None, leaf, None, "panel")),
        check_vma=False,
    )
```

```python
import functools

import jax
import jax.numpy as jnp
from jax import lax
from jax.experimental import pallas as pl
from jax.experimental.pallas import tpu as pltpu
from jax.sharding import Mesh, PartitionSpec as P

BF = jnp.bfloat16
F32 = jnp.float32
GROUP = 8
VMEM = pl.BlockSpec(memory_space=pltpu.VMEM)
SMEM = pl.BlockSpec(memory_space=pltpu.SMEM)
HBM = pl.BlockSpec(memory_space=pltpu.HBM)
PARAMS = pltpu.CompilerParams(vmem_limit_bytes=8 * 1024 * 1024)
NT = (((1,), (1,)), ((), ()))
NN = (((1,), (0,)), ((), ()))


def mul_t(a, b):
    return lax.dot_general(a, b, NT, preferred_element_type=F32)


def mul(a, b):
    return lax.dot_general(a, b, NN, preferred_element_type=F32)


def call(body, outs, *args, specs=None, outs_at=VMEM, scratch=()):
    specs = [VMEM] * len(args) if specs is None else specs
    args = [far(x) if spec is HBM else x for x, spec in zip(args, specs)]
    return pl.pallas_call(
        body,
        out_shape=tuple(outs) if isinstance(outs, list) else outs,
        in_specs=specs,
        out_specs=outs_at if isinstance(outs_at, list) else jax.tree.map(lambda _: outs_at, outs),
        scratch_shapes=list(scratch),
        compiler_params=PARAMS,
    )(*args)


def far(x):
    return pltpu.with_memory_space_constraint(x, pltpu.HBM)


def sds(*shape, dtype=BF):
    return jax.ShapeDtypeStruct(shape, dtype)


def leaf_place():
    z = lax.axis_index("z")
    lane = lax.axis_index("x") * lax.axis_size("core") + lax.axis_index("core")
    return z, lane, z * GROUP + lane


def order(k, panels):
    return lax.rem(lax.axis_index("panel") + panels - k, panels)


def pack_body(rhs, coupling, own, beside, *refs):
    *outs, sems = refs
    panels = len(outs) + 1
    rows, quarter = rhs.shape[2:]
    width = coupling.shape[-1]
    pairs = []
    for k, out in enumerate((own, *outs)):
        target = lax.rem(lax.axis_index("panel") + k, panels)
        start = pl.multiple_of(target * quarter, quarter)
        source = coupling.at[0, 0, pl.ds(start, quarter)]
        if k == 0:
            pairs.append((source, out))
            continue
        pairs.append((source, out.at[pl.ds(2 * rows, quarter)]))
        for half in range(2):
            lanes = pl.ds(half * width, width)
            pairs.append((rhs.at[0, 0, :, lanes], out.at[pl.ds(half * rows, rows)]))
    for part in range(panels):
        source = coupling.at[1, 0, pl.ds(part * quarter, quarter)]
        pairs.append((source, beside.at[:, pl.ds(part * width, width)]))
    copies = [pltpu.make_async_copy(a, b, sems.at[i]) for i, (a, b) in enumerate(pairs)]
    for copy in copies:
        copy.start()
    for copy in copies:
        copy.wait()


def last_weights_body(coupling, inv, *refs):
    *outs, sems = refs
    rows = inv.shape[2]
    width = coupling.shape[-1]
    parts = len(outs)
    copies = []
    for k, out in enumerate(outs):
        target = lax.rem(lax.axis_index("panel") + k, parts)
        for part in range(parts):
            source = coupling.at[0, 0, pl.ds(part * rows, rows)]
            copies.append((source, out.at[:, pl.ds(part * width, width)]))
        cols = pl.ds(pl.multiple_of(target * rows, rows), rows)
        for start in range(parts * width, out.shape[1], rows):
            copies.append((inv.at[0, 0, :, cols], out.at[:, pl.ds(start, rows)]))
    copies = [pltpu.make_async_copy(a, b, sems.at[i]) for i, (a, b) in enumerate(copies)]
    for copy in copies:
        copy.start()
    for copy in copies:
        copy.wait()


def first_body(rhs, own, m1, m2, m3, inv, send):
    panels = send.shape[0]
    rows, quarter = rhs.shape[2:]
    total = None
    for k, ref in enumerate((rhs, m1, m2, m3)):
        q = order(k, panels)
        block = rhs[0, 0] if k == 0 else jnp.concatenate([ref[:rows], ref[rows : 2 * rows]], axis=1)
        part = mul_t(block, inv[:, pl.ds(pl.multiple_of(q * quarter, quarter), quarter)])
        total = part if total is None else total + part
    f = total.astype(BF)
    few = rows // panels
    for k, ref in enumerate((own, m1, m2, m3)):
        q = order(k, panels)
        part = mul(f, own[...] if k == 0 else ref[2 * rows :])
        high = part.astype(BF)
        low = (part - high.astype(F32)).astype(BF)
        for d in range(panels):
            send[d, q] = high[d * few : (d + 1) * few]
            send[d, panels + q] = low[d * few : (d + 1) * few]
    for d in range(panels):
        span = slice(d * few, (d + 1) * few)
        for index, value in enumerate((f[span], rhs[1, 0, span], rhs[2, 0, span])):
            send[d, 2 * panels + 2 * index] = value[:, :128]
            send[d, 2 * panels + 2 * index + 1] = value[:, 128:]


def place(level, counts, lists, rows):
    _, _, leaf = leaf_place()
    mine = lists[level, pl.ds(leaf, 1), :]
    shape = (rows, lists.shape[-1])
    row = lax.broadcasted_iota(jnp.int32, shape, 0)
    col = lax.broadcasted_iota(jnp.int32, shape, 1)
    return jnp.where((row == mine) & (col < counts[level, leaf]), 1.0, 0.0).astype(BF)


def laid_out(level, u, placed, counts):
    _, _, leaf = leaf_place()
    col = lax.broadcasted_iota(jnp.int32, u.shape, 1)
    u = jnp.where(col < counts[level, leaf], u, 0.0).astype(BF)
    return mul_t(u, placed).astype(BF)


def whole(got, index):
    panels = got.shape[0]
    first = 2 * panels + 2 * index
    return jnp.concatenate(
        [got[q, first + half] for q in range(panels) for half in range(2)], axis=1
    )


def up0_body(counts, got, lists, inv, out, share, sem):
    copy = pltpu.make_async_copy(inv.at[1, 0], share, sem)
    copy.start()
    placed = place(0, counts, lists, out.shape[2])
    panels = got.shape[0]
    pieces = []
    for q in range(panels):
        total = None
        for source in range(panels):
            part = got[source, q].astype(F32) + got[source, panels + q].astype(F32)
            total = part if total is None else total + part
        pieces.append(total)
    e = laid_out(0, jnp.concatenate(pieces, axis=1), placed, counts)
    for d in range(out.shape[0]):
        out[d] = e
    copy.wait()


def summed(recv):
    total = recv[0].astype(F32)
    for j in range(1, recv.shape[0]):
        total = total + recv[j].astype(F32)
    return total


def forward(resid, blocks, out):
    rows, cols = blocks[0].shape[0], out.shape[1]
    for k, ref in enumerate(blocks):
        start = pl.multiple_of(order(k, len(blocks)) * rows, rows)
        out[:, pl.ds(start, rows)] = mul_t(resid, ref[:, :cols]).astype(BF)
    return out[...]


def backward(reduced, blocks):
    rows, cols = blocks[0].shape[0], reduced.shape[1]
    total = None
    for k, ref in enumerate(blocks):
        start = pl.multiple_of(order(k, len(blocks)) * rows, rows)
        part = mul(reduced[:, pl.ds(start, rows)], ref[:, :cols])
        total = part if total is None else total + part
    return total.astype(BF)


def coupled(f, blocks, first, out):
    rows = blocks[0].shape[0]
    parts = f.shape[1] // rows
    width = out.shape[1] // len(blocks)
    for k, ref in enumerate(blocks):
        total = None
        for part in range(parts):
            lanes = slice(first + part * width, first + (part + 1) * width)
            term = mul(f[:, part * rows : (part + 1) * rows], ref[:, lanes])
            total = term if total is None else total + term
        out[:, pl.ds(pl.multiple_of(order(k, len(blocks)) * width, width), width)] = total


def lessened(level, f, recv, parents, placed, blocks, first, picked, place_of):
    _, _, leaf = leaf_place()
    above = recv[lax.rem(parents[level, leaf], GROUP)]
    picked[...] = mul(above, placed).astype(BF)
    rows = blocks[0].shape[0]
    width = picked.shape[1] // len(blocks)
    pieces = []
    for part in range(f.shape[1] // rows):
        lanes = slice(first + part * width, first + (part + 1) * width)
        total = None
        for k, ref in enumerate(blocks):
            start = pl.multiple_of(place_of(k) * width, width)
            term = mul_t(picked[:, pl.ds(start, width)], ref[:, lanes])
            total = term if total is None else total + term
        pieces.append(total)
    return (f.astype(F32) - jnp.concatenate(pieces, axis=1)).astype(BF)


def to_all(out, value):
    for d in range(out.shape[0]):
        out[d] = value


def up1_body(counts, recv, got, lists, i0, i1, i2, i3, c0, c1, c2, c3, fout, out, keep, scratch, sems):
    inverse, blocks = (i0, i1, i2, i3), (c0, c1, c2, c3)
    cols = i0.shape[1]
    copies = []
    for k in range(len(blocks)):
        for part, (source, span) in enumerate(
            ((inverse[k], pl.ds(0, cols)), (blocks[k], pl.ds(cols, c0.shape[1])))
        ):
            target = keep.at[order(k, len(blocks)), :, span]
            copies.append(pltpu.make_async_copy(source, target, sems.at[k, part]))
    for copy in copies:
        copy.start()
    resid = (whole(got, 1).astype(F32) - summed(recv)).astype(BF)
    placed = place(1, counts, lists, fout.shape[1])
    f = forward(resid, inverse, fout)
    coupled(f, blocks, 0, scratch)
    to_all(out, laid_out(1, scratch[...], placed, counts))
    for copy in copies:
        copy.wait()


def top_body(recv, got, i0, i1, i2, i3, fout, out):
    resid = (whole(got, 2).astype(F32) - summed(recv)).astype(BF)
    blocks = (i0, i1, i2, i3)
    forward(resid, blocks, fout)
    to_all(out, backward(fout, blocks))


def fold_body(level, parents, blocks, out, acc):
    z, lane, _ = leaf_place()
    acc[...] = jnp.zeros_like(acc)
    for j in range(blocks.shape[0]):
        parent = parents[level, j * GROUP + lane]
        d = jnp.where(lax.div(parent, GROUP) == z, lax.rem(parent, GROUP), GROUP)
        acc[d] = acc[d] + blocks[j].astype(F32)
    for d in range(out.shape[0]):
        out[d] = acc[d].astype(BF)


def route_body(level, parents, blocks, out):
    z, _, _ = leaf_place()
    for d in range(out.shape[0]):
        out[d] = blocks[lax.div(parents[level, z * GROUP + d], GROUP)]


def down1_body(parents, counts, recv, f, lists, keep, out, picked, red, held, sems):
    cols = red.shape[1]
    rows = keep.shape[1]
    panels = keep.shape[0]

    def copy(q, part, span):
        return pltpu.make_async_copy(keep.at[q, :, span], held.at[q, :, span], sems.at[q, part])

    couplings = [copy(q, 0, pl.ds(cols, held.shape[2] - cols)) for q in range(panels)]
    inverse = [copy(q, 1, pl.ds(0, (q + 1) * rows)) for q in range(panels)]
    for started in couplings + inverse:
        started.start()
    blocks = [held.at[q] for q in range(panels)]
    placed = place(1, counts, lists, cols)
    for started in couplings:
        started.wait()
    red[...] = lessened(1, f[...], recv, parents, placed, blocks, cols, picked, lambda q: q)
    for started in inverse:
        started.wait()
    pieces = []
    for part in range(panels):
        lanes = slice(part * rows, (part + 1) * rows)
        total = None
        for q in range(part, panels):
            term = mul(red[:, q * rows : (q + 1) * rows], held[q, :, lanes])
            total = term if total is None else total + term
        pieces.append(total)
    to_all(out, jnp.concatenate(pieces, axis=1).astype(BF))


def down0_body(
    parents, counts, recv, got, lists, b0, b1, b2, b3, f1, f2, s2, s1,
    o0, o1, o2, o3, scratch, f0,
):
    outs = (o0, o1, o2, o3)
    width = f1.shape[1]
    quarter = width // len(outs)
    f0[...] = whole(got, 0)
    placed = place(0, counts, lists, width)
    red = lessened(0, f0[...], recv, parents, placed, (b0, b1, b2, b3), 0, scratch,
        lambda k: order(k, 4),
    )
    for k, out in enumerate(outs):
        target = lax.rem(lax.axis_index("panel") + k, len(outs))
        cols = pl.ds(pl.multiple_of(target * quarter, quarter), quarter)
        out[:, :width] = red
        for index, value in enumerate(
            (f0[:, cols], f1[:, cols], f2[:, cols], s2[0, :, cols], s1[0, :, cols])
        ):
            out[:, width + index * quarter : width + (index + 1) * quarter] = value


def last_body(*refs):
    panels = (len(refs) - 3) // 2
    ends, cols = refs[:panels], refs[panels : 2 * panels]
    first = cols[0].shape[1] - cols[0].shape[0]
    fwd, sol, reds = refs[2 * panels :]
    width = reds.shape[1]
    quarter = width // panels
    rows = ends[0].shape[0]
    for k in range(panels):
        q = order(k, panels)
        span = pl.ds(pl.multiple_of(q * rows, rows), rows)
        reds[span] = ends[k][:, :width]
        for index, (out, level) in enumerate(
            ((fwd, 0), (fwd, 1), (fwd, 2), (sol, 2), (sol, 1))
        ):
            out[level, 0, span] = ends[k][:, width + index * quarter : width + (index + 1) * quarter]
    total = None
    for k in range(panels):
        q = order(k, panels)
        part = mul(
            reds[:, pl.ds(pl.multiple_of(q * quarter, quarter), quarter)], cols[k][:, first : first + quarter]
        )
        total = part if total is None else total + part
    sol[0, 0] = total.astype(BF)


def local(rhs, inv_diag, coupling, row_lists, parents, counts):
    panels = lax.axis_size("panel")
    rows = rhs.shape[2] // panels
    mid = (GROUP, rows, inv_diag.shape[3])
    after = lax.optimization_barrier

    def shifted(x, k):
        return lax.ppermute(x, "panel", [(i, (i + k) % panels) for i in range(panels)])

    half = coupling.shape[3]
    tall = rhs.shape[3]
    half = coupling.shape[3]
    tall = rhs.shape[3]
    width = inv_diag.shape[3]

    def exchange(x, axes, weights=(), shifts=()):
        x, *weights = after((x, *weights))
        moved = [shifted(w, k) for w, k in zip(weights, shifts)]
        x = lax.all_to_all(x, axes, 0, 0)
        return after((x, *moved))

    own, c1, *packs = call(
        pack_body,
        [sds(tall, half), sds(tall, panels * half)]
        + [sds(2 * rhs.shape[2] + tall, half)] * (panels - 1),
        rhs, coupling, specs=[HBM] * 2,
        scratch=[pltpu.SemaphoreType.DMA((4 * panels - 2,))],
    )
    packs = [shifted(x, k) for k, x in enumerate(packs, 1)]
    base, in2 = inv_diag[0, 0], inv_diag[2, 0]
    packs[0], c1 = after((packs[0], c1))
    c11, c12, c13 = (shifted(c1, k) for k in range(1, panels))
    base, in2 = after((base, in2))
    send = call(
        first_body, sds(panels, 14, rows, half), rhs, own, *packs, base,
    )
    got = lax.all_to_all(send, "panel", 0, 0)
    got, c11, c12, c13 = after((got, c11, c12, c13))
    touched = pltpu.VMEM((rows, panels * half), BF)
    wide = pltpu.VMEM((rows, panels * half), F32)
    e, in1 = call(
        up0_body, [sds(*mid), sds(*inv_diag.shape[2:])], counts, got, row_lists, inv_diag,
        specs=[SMEM] + [VMEM] * 2 + [HBM], outs_at=[VMEM, HBM],
        scratch=[pltpu.SemaphoreType.DMA],
    )

    def fold(e, level, table):
        return call(
            functools.partial(fold_body, level), sds(*mid), table, e,
            specs=[SMEM, VMEM], scratch=[pltpu.VMEM((GROUP + 1, *mid[1:]), F32)],
        )

    def route(s, level, table):
        return call(functools.partial(route_body, level), sds(*mid), table, s, specs=[SMEM, VMEM])

    e, in11, in13 = exchange(e, "z", [in1, in1], [1, 3])
    e = fold(e, 0, parents)
    e, in12 = exchange(e, ("x", "core"), [in1], [2])
    level1 = (in1, in11, in12, in13, c1, c11, c12, c13)
    f1, e, keep = call(
        up1_body, [sds(*mid[1:]), sds(*mid), sds(panels, tall, width + panels * half)],
        counts, e, got, row_lists, *level1,
        specs=[SMEM] + [VMEM] * 11, outs_at=[VMEM, VMEM, HBM],
        scratch=[wide, pltpu.SemaphoreType.DMA((panels, 2))],
    )
    e, in21, in23 = exchange(e, "z", [in2, in2], [1, 3])
    e = fold(e, 1, parents)
    e, in22 = exchange(e, ("x", "core"), [in2], [2])
    f2, s2 = call(
        top_body, (sds(*mid[1:]), sds(*mid)), e, got, in2, in21, in22, in23
    )
    s, inv_late, near_coupling = after((s2, inv_diag, coupling))
    w0 = call(
        last_weights_body,
        [sds(tall, panels * half + (2 if k == 2 else 1) * tall) for k in range(panels)],
        near_coupling, inv_late,
        specs=[HBM] * 2, outs_at=HBM,
        scratch=[pltpu.SemaphoreType.DMA((panels * (panels + 1) + 1,))],
    )
    w0 = [*w0]
    s = lax.all_to_all(s, "z", 0, 0)
    w01, w03 = shifted(w0[1], 1), shifted(w0[3], 3)
    s, w0[0], w0[2] = after((s, w0[0], w0[2]))
    s = route(s, 1, parents)
    s = lax.all_to_all(s, ("x", "core"), 0, 0)
    s, w01, w03 = after((s, w01, w03))
    s1 = call(
        down1_body, sds(*mid), parents, counts, s, f1, row_lists, keep,
        specs=[SMEM] * 2 + [VMEM] * 3 + [HBM],
        scratch=[
            touched, pltpu.VMEM(mid[1:], BF), pltpu.VMEM(keep.shape, BF),
            pltpu.SemaphoreType.DMA((panels, 2)),
        ],
    )
    s, w02 = exchange(s1, "z", [w0[2]], [2])
    w0 = (w0[0], w01, w02, w03)
    s = route(s, 0, parents)
    s = lax.all_to_all(s, ("x", "core"), 0, 0)
    ends = call(
        down0_body, [sds(rows, mid[2] + 5 * tall)] * panels,
        parents, counts, s, got, row_lists, *w0, f1, f2, s2, s1,
        specs=[SMEM] * 2 + [VMEM] * 11, scratch=[touched, pltpu.VMEM(mid[1:], BF)],
    )
    ends = [ends[0]] + [shifted(x, k) for k, x in enumerate(ends[1:], 1)]
    return call(
        last_body, (sds(*rhs.shape), sds(*rhs.shape)), *ends, *w0,
        scratch=[pltpu.VMEM((rhs.shape[2], mid[2]), BF)],
    )


def solution(mesh):
    leaves, panels = mesh.shape["leaf"], mesh.shape["panel"]
    inner = Mesh(
        mesh.devices.reshape(leaves // GROUP, GROUP // 2, 2, panels), ("z", "x", "core", "panel")
    )
    leaf = ("z", "x", "core")
    placed = (
        P(None, leaf, None, "panel"),
        P(None, leaf, "panel", None),
        P(None, leaf, None, "panel"),
        P(),
        P(),
        P(),
    )
    return jax.shard_map(
        local,
        mesh=inner,
        in_specs=placed,
        out_specs=(P(None, leaf, None, "panel"), P(None, leaf, None, "panel")),
        check_vma=False,
    )
```
